32 devices in a mesh: groups: 2 (over y), patch: 4 (over z), head: 4 (over x, core).
Axes of the slice: x: 2, y: 2, z: 4, core: 2. Of those that a mesh axis runs over, the one named last changes fastest.
Arguments:
- queries: bfloat16 [1536, 1536], P(('groups', 'patch'), 'head'), parts along dimension 0, may hold values from -12.5 to 12.5
- fresh_keys: bfloat16 [1536, 1536], P(('groups', 'patch'), 'head'), parts along dimension 0, may hold values from -5 to 5
- fresh_values: bfloat16 [1536, 1536], P(('groups', 'patch'), 'head'), parts along dimension 0, may hold values from -6 to 6
- stale_keys: bfloat16 [1536, 1536], P(('groups', 'patch'), 'head'), parts along dimension 0, may hold values from -5 to 5
- stale_values: bfloat16 [1536, 1536], P(('groups', 'patch'), 'head'), parts along dimension 0, may hold values from -6 to 6
- out_weight: bfloat16 [1536, 5120], P('head', 'patch'), may hold values from -0.21875 to 0.21875
- gate_scale: float32 [10240], P(('groups', 'head')), parts along dimension 0, may hold values from 1 to 4
Outputs:
- branch_out: float32 [1536, 5120], P(('groups', 'patch'), 'head'), parts along dimension 0
The draws below stay inside these ranges and needn't reach their ends.
There are 2 independent parts, one for each index of `groups`. The reference program is written for one: setup_inputs(seed, part) draws one part's arguments, and reference() takes and returns one part's arrays. A program takes and returns all parts, laid end to end along the dimension named above; an argument that names none is the same for every part. Nothing has to cross between parts.
All inputs are finite; a program needn't handle non-finite values.
Results may differ from the reference program's by a relative error of at most 0.006.
Values may be sent and summed in bfloat16 or wider, within the bound.
A program may use at most 64 MiB of HBM per device.

```python
import math
import jax
import jax.numpy as jnp
from jax import lax

D = 5120
HEAD_DIM = 128
HEAD_DEV = 3
TOK_DEV = 192
HEADS = 12
TOKENS = 768
N_PATCH = 4
N_HEAD = 4


def attention_inputs(key):
    feature_width = HEADS * HEAD_DIM
    key_query, key_stale, key_fresh = jax.random.split(jax.random.fold_in(key, 7), 3)
    shape = (TOKENS, feature_width)
    query_rows = 2.5 * jax.random.truncated_normal(key_query, -5.0, 5.0, shape, jnp.float32)
    stale_rows = jax.random.truncated_normal(key_stale, -5.0, 5.0, shape, jnp.float32)
    fresh_rows = jnp.clip(0.8 * stale_rows + 0.6 * jax.random.normal(key_fresh, shape, jnp.float32), -5.0, 5.0)
    return (query_rows, stale_rows, fresh_rows)


def draw_queries(key, part):
    return attention_inputs(key)[0].astype(jnp.bfloat16)


def draw_stale_keys(key, part):
    return attention_inputs(key)[1].astype(jnp.bfloat16)


def draw_fresh_keys(key, part):
    return attention_inputs(key)[2].astype(jnp.bfloat16)


def spiked(values, rng, source, target, blocks, factor):
    owner, partner = [(jnp.arange(values.shape[dim]) // (values.shape[dim] // blocks)).reshape([-1 if axis == dim else 1 for axis in range(values.ndim)]) for dim in (source, target)]
    chosen = jax.random.permutation(rng, blocks)[partner]
    strong = (owner == chosen) | (owner == (partner + blocks // 2) % blocks)
    return jnp.where(strong, factor * values, values)


def steps_of(key, shape, cuts, low, top_value):
    factor_of = 1.0
    for position, shards_of in cuts:
        steps = jax.random.uniform(jax.random.fold_in(jax.random.fold_in(key, 6), position), (shards_of,), jnp.float32, low / len(cuts), top_value / len(cuts))
        factor_of = factor_of * jnp.repeat(jnp.exp(steps), shape[position] // shards_of).reshape((-1,) + (1,) * (len(shape) - 1 - position))
    return factor_of


def normal_values(rng, dims, deviation, limit, shards=(), held_as=jnp.bfloat16):
    drawn = deviation * jax.random.normal(rng, dims, jnp.float32)
    if shards:
        drawn = drawn * steps_of(rng, dims, shards, -0.22, 0.18)
    return jnp.clip(drawn, -limit, limit).astype(held_as)


def heavy_noise(stream_key, extent, deviation, reach, pieces, heavy, held_as=jnp.bfloat16):
    entries = deviation * jax.random.normal(stream_key, extent, jnp.float32)
    if pieces:
        entries = entries * steps_of(stream_key, extent, pieces, -0.22, 0.18)
    return jnp.clip(spiked(entries, jax.random.fold_in(stream_key, 3), *heavy), -reach, reach).astype(held_as)


def setup_inputs(seed: int = 0, part: int = 0) -> dict:
    arg_keys = jax.random.split(jax.random.key(seed), 8)
    own_keys = jax.random.split(jax.random.fold_in(arg_keys[7], part), 8)
    queries = draw_queries(jax.random.fold_in(jax.random.fold_in(arg_keys[7], part), 71), part)
    fresh_keys = draw_fresh_keys(jax.random.fold_in(jax.random.fold_in(arg_keys[7], part), 71), part)
    fresh_values = normal_values(own_keys[2], (TOKENS, HEADS * HEAD_DIM), 1.0, 6.0, ((0, 4), (1, 4)))
    stale_keys = draw_stale_keys(jax.random.fold_in(jax.random.fold_in(arg_keys[7], part), 71), part)
    stale_values = normal_values(own_keys[4], (TOKENS, HEADS * HEAD_DIM), 1.0, 6.0, ((0, 4), (1, 4)))
    out_weight = heavy_noise(arg_keys[5], (HEADS * HEAD_DIM, D), (HEADS * HEAD_DIM) ** -0.5, 0.21875, ((0, 4), (1, 4)), (0, 1, 4, 2.0))
    gate_scale = jnp.clip(jnp.exp(math.log(4.0) - 1.3862944 * jax.random.uniform(own_keys[6], (D,), jnp.float32) ** steps_of(own_keys[6], (D,), ((0, 4),), -0.2, 0.2)), 1.0, 4.0)
    return dict(queries=queries, fresh_keys=fresh_keys, fresh_values=fresh_values, stale_keys=stale_keys, stale_values=stale_values, out_weight=out_weight, gate_scale=gate_scale)


def reference(queries, fresh_keys, fresh_values, stale_keys, stale_values, out_weight, gate_scale):
    query_heads = queries.astype(jnp.float32).reshape(TOKENS, HEADS, HEAD_DIM)

    def one_slab(slab):
        anchor = (slab * TOK_DEV).astype(jnp.int32)
        query_rows = lax.dynamic_slice_in_dim(query_heads, anchor, TOK_DEV, 0)
        key_rows = lax.dynamic_slice_in_dim(fresh_keys, anchor, TOK_DEV, 0)
        value_rows = lax.dynamic_slice_in_dim(fresh_values, anchor, TOK_DEV, 0)
        keys_used = lax.dynamic_update_slice_in_dim(stale_keys, key_rows, anchor, 0)
        values_used = lax.dynamic_update_slice_in_dim(stale_values, value_rows, anchor, 0)
        key_heads = keys_used.astype(jnp.float32).reshape(TOKENS, HEADS, HEAD_DIM)
        value_heads = values_used.astype(jnp.float32).reshape(TOKENS, HEADS, HEAD_DIM)
        scores = jnp.einsum("qhd,khd->hqk", query_rows, key_heads) * (HEAD_DIM ** -0.5)
        top = jnp.max(scores, axis=2)
        weights = jnp.exp(scores - top[:, :, None])
        total = jnp.sum(weights, axis=2)
        rounded = lax.optimization_barrier(weights.astype(jnp.bfloat16)).astype(jnp.float32)
        mixture = jnp.einsum("hqk,khd->qhd", rounded, value_heads)
        return (mixture / jnp.transpose(total)[:, :, None]).astype(jnp.bfloat16)

    attended = lax.map(one_slab, jnp.arange(N_PATCH, dtype=jnp.int32))
    attended = attended.reshape(TOKENS, HEADS * HEAD_DIM)
    group_width = HEAD_DEV * HEAD_DIM

    def add_group(running, group):
        anchor = (group * group_width).astype(jnp.int32)
        column_block = lax.dynamic_slice_in_dim(attended, anchor, group_width, 1)
        weight_block = lax.dynamic_slice_in_dim(out_weight, anchor, group_width, 0)
        term = jnp.dot(column_block, weight_block, preferred_element_type=jnp.float32)
        return running + term, None

    summed, unused = lax.scan(add_group, jnp.zeros((TOKENS, D), jnp.float32), jnp.arange(N_HEAD, dtype=jnp.int32))
    return gate_scale[None, :] * summed
```

```python
import functools

import jax
import jax.numpy as jnp
from jax import lax
from jax.experimental import pallas as pl
from jax.experimental.pallas import tpu as pltpu
from jax.sharding import PartitionSpec as P

HEAD_DIM = 128
MESH = pl.DeviceIdType.MESH
CORES = 2


neg_large = -1e30


def head_view(matrix):
    return matrix.reshape(matrix.shape[0], -1, HEAD_DIM)


def block_scores(query_heads, key_block):
    return jnp.einsum(
        "qhd,khd->hqk", query_heads, head_view(key_block), preferred_element_type=jnp.float32
    ) * HEAD_DIM ** (-0.5)


def absorb(running, scores, value_block):
    run_max, run_total, run_acc = running
    new_max = jnp.maximum(run_max, jnp.max(scores, axis=2))
    factor = jnp.exp(run_max - new_max)
    weights = jnp.exp(scores - new_max[:, :, None])
    new_total = run_total * factor + jnp.sum(weights, axis=2)
    mixture = jnp.einsum(
        "hqk,khd->qhd",
        weights.astype(jnp.bfloat16),
        head_view(value_block),
        preferred_element_type=jnp.float32,
    )
    new_acc = run_acc * jnp.transpose(factor)[:, :, None] + mixture
    return (new_max, new_total, new_acc)


def empty_state(row_count, head_count):
    return (
        jnp.full((head_count, row_count), neg_large, jnp.float32),
        jnp.zeros((head_count, row_count), jnp.float32),
        jnp.zeros((row_count, head_count, HEAD_DIM), jnp.float32),
    )


def sublayer_kernel(
    n_patch, n_head, q_ref, fk_ref, fv_ref, sk_ref, sv_ref, w_ref, out_ref,
    kbuf, vbuf, wsub, wbuf, abuf, ostage, obuf, top, total, acc,
    kv_send, kv_recv, w_send, w_recv, z_send, x_send, sib_send, a_recv, o_send, o_recv,
):
    g, p, h = lax.axis_index("groups"), lax.axis_index("patch"), lax.axis_index("head")
    core, chip = lax.rem(h, CORES), lax.div(h, CORES)
    sibling = h + 1 - 2 * core
    sub = wsub.shape[2]
    heads = q_ref.shape[1] // HEAD_DIM
    scale = HEAD_DIM ** (-0.5)

    barrier = pltpu.get_barrier_semaphore()
    for s in range(n_patch):
        for j in range(n_head):
            @pl.when(jnp.logical_or(p != s, h != j))
            def _():
                pl.semaphore_signal(barrier, inc=1, device_id=(g, s, j), device_id_type=MESH)
    for j in range(n_head):
        wsub[j] = w_ref[:, j * sub:(j + 1) * sub]
    wbuf[h] = wsub[h]
    pl.semaphore_wait(barrier, n_patch * n_head - 1)

    def remote(src, dst, send, recv, patch, head):
        return pltpu.make_async_remote_copy(
            src_ref=src, dst_ref=dst, send_sem=send, recv_sem=recv,
            device_id=(g, patch, head), device_id_type=MESH,
        )

    def neighbour(side):
        return p + 1 - 2 * side

    def has_neighbour(side):
        return (p < n_patch - 1) if side == 0 else (p > 0)

    def slab_at(side, d):
        return p - d if side == 0 else p + d

    def is_slab(side, d):
        return (p - d >= 0) if side == 0 else jnp.logical_and(p + d < n_patch, d >= 1)

    def kv_copy(side, which, s, src):
        buf = (kbuf, vbuf)[which]
        return remote(
            src, buf.at[s], kv_send.at[side, which, s], kv_recv.at[which, s], neighbour(side), h
        )

    for which, src in ((0, sk_ref), (1, sv_ref)):
        for side in range(2):
            @pl.when(has_neighbour(side))
            def _():
                kv_copy(side, which, p, src).start()

    def w_copy(j):
        return remote(wsub.at[j], wbuf.at[h], w_send.at[j], w_recv.at[h], p, j)

    for j in range(n_head):
        @pl.when(h != j)
        def _():
            w_copy(j).start()

    def absorb_block(keys, values, first):
        for i in range(heads):
            cols = slice(i * HEAD_DIM, (i + 1) * HEAD_DIM)
            scores = lax.dot_general(
                q_ref[:, cols], keys[:, cols], (((1,), (1,)), ((), ())),
                preferred_element_type=jnp.float32,
            )
            new_top = jnp.max(scores, axis=1, keepdims=True)
            if not first:
                old_top = top[i]
                new_top = jnp.maximum(old_top, new_top)
                factor = jnp.exp((old_top - new_top) * scale)
            weights = jnp.exp((scores - new_top) * scale)
            new_total = jnp.sum(weights, axis=1, keepdims=True)
            mixture = jnp.dot(
                weights.astype(jnp.bfloat16), values[:, cols], preferred_element_type=jnp.float32
            )
            if not first:
                new_total = new_total + total[i] * factor
                mixture = mixture + acc[i] * factor
            top[i] = new_top
            total[i] = new_total
            acc[i] = mixture

    absorb_block(fk_ref[...], fv_ref[...], True)

    def kv_step(d, carry):
        for which in range(2):
            for side in range(2):
                s = slab_at(side, d)

                @pl.when(is_slab(side, d))
                def _():
                    buf = (kbuf, vbuf)[which]
                    copy = kv_copy(side, which, s, buf.at[s])
                    copy.wait_recv()

                    @pl.when(has_neighbour(side))
                    def _():
                        copy.start()
        for side in range(2):
            s = slab_at(side, d)

            @pl.when(is_slab(side, d))
            def _():
                absorb_block(kbuf.at[s][...], vbuf.at[s][...], False)
        return carry

    lax.fori_loop(1, n_patch, kv_step, 0)

    for i in range(heads):
        abuf[p, h, :, i * HEAD_DIM:(i + 1) * HEAD_DIM] = (acc[i] / total[i]).astype(jnp.bfloat16)

    def z_copy(side, s):
        return remote(
            abuf.at[s, h], abuf.at[s, h], z_send.at[side, s], a_recv.at[s, h], neighbour(side), h
        )

    def x_copy(xx, s):
        return remote(
            abuf.at[s, h], abuf.at[s, h], x_send.at[xx, s], a_recv.at[s, h], p, xx * CORES + core
        )

    def sib_copy(s, head):
        return remote(
            abuf.at[s, head], abuf.at[s, head], sib_send.at[s, head], a_recv.at[s, head], p, sibling
        )

    def spread(s):
        for xx in range(n_head // CORES):
            @pl.when(chip != xx)
            def _():
                x_copy(xx, s).start()
        sib_copy(s, h).start()

    for side in range(2):
        @pl.when(has_neighbour(side))
        def _():
            z_copy(side, p).start()
    spread(p)

    for j in range(n_head):
        @pl.when(h != j)
        def _():
            remote(wsub.at[j], wbuf.at[j], w_send.at[j], w_recv.at[j], p, j).wait_recv()

    def o_copy(s):
        return remote(ostage.at[s], obuf.at[h], o_send.at[s], o_recv.at[h], s, p)

    def stays(s):
        return jnp.logical_and(s == p, h == p)

    def project(s):
        for xx in range(n_head // CORES):
            head = xx * CORES + 1 - core
            sib_in = remote(
                abuf.at[s, head], abuf.at[s, head], sib_send.at[s, h], a_recv.at[s, head], p, sibling
            )
            sib_in.wait_recv()
        term = jnp.dot(abuf[s, 0], wbuf[0], preferred_element_type=jnp.float32)
        for j in range(1, n_head):
            term = term + jnp.dot(abuf[s, j], wbuf[j], preferred_element_type=jnp.float32)
        ostage[s] = term.astype(jnp.bfloat16)

        @pl.when(stays(s))
        def _():
            obuf[h] = ostage[s]

        @pl.when(jnp.logical_not(stays(s)))
        def _():
            o_copy(s).start()

    def spread_step(d, carry):
        for side in range(2):
            s = slab_at(side, d)

            @pl.when(is_slab(side, d))
            def _():
                copy = z_copy(side, s)
                copy.wait_recv()

                @pl.when(has_neighbour(side))
                def _():
                    copy.start()
                spread(s)
        for side in range(2):
            s = slab_at(side, d - 1)

            @pl.when(is_slab(side, d - 1))
            def _():
                for xx in range(n_head // CORES):
                    @pl.when(chip != xx)
                    def _():
                        head = xx * CORES + core
                        remote(
                            abuf.at[s, head], abuf.at[s, head], x_send.at[xx, s],
                            a_recv.at[s, head], p, head,
                        ).wait_recv()
                        sib_copy(s, head).start()
        for side in range(2):
            s = slab_at(side, d - 1)

            @pl.when(is_slab(side, d - 1))
            def _():
                project(s)
        return carry

    lax.fori_loop(1, n_patch + 1, spread_step, 0)

    for j in range(n_head):
        @pl.when(jnp.logical_or(p != h, h != j))
        def _():
            remote(ostage.at[0], obuf.at[j], o_send.at[0], o_recv.at[j], h, j).wait_recv()
        out_ref[:, j * sub:(j + 1) * sub] = obuf[j]

    for j in range(n_head):
        @pl.when(h != j)
        def _():
            w_copy(j).wait_send()

    def drain(s, carry):
        for side in range(2):
            passes = (s <= p) if side == 0 else (s >= p)

            @pl.when(jnp.logical_and(passes, has_neighbour(side)))
            def _():
                kv_copy(side, 0, s, kbuf.at[s]).wait_send()
                kv_copy(side, 1, s, vbuf.at[s]).wait_send()
                z_copy(side, s).wait_send()
        for xx in range(n_head // CORES):
            @pl.when(chip != xx)
            def _():
                x_copy(xx, s).wait_send()
            sib_copy(s, xx * CORES + core).wait_send()

        @pl.when(jnp.logical_not(stays(s)))
        def _():
            o_copy(s).wait_send()
        return carry

    lax.fori_loop(0, n_patch, drain, 0)


def fused_sublayer(n_patch, n_head, queries, fresh_keys, fresh_values, stale_keys, stale_values, out_weight):
    rows, width = queries.shape
    columns = out_weight.shape[1]
    sub = columns // n_head
    heads = width // HEAD_DIM
    bf16, dma = jnp.bfloat16, pltpu.SemaphoreType.DMA
    return pl.pallas_call(
        functools.partial(sublayer_kernel, n_patch, n_head),
        out_shape=jax.ShapeDtypeStruct((rows, columns), bf16),
        in_specs=[pl.BlockSpec(memory_space=pltpu.VMEM)] * 6,
        out_specs=pl.BlockSpec(memory_space=pltpu.VMEM),
        scratch_shapes=[
            pltpu.VMEM((n_patch, rows, width), bf16),
            pltpu.VMEM((n_patch, rows, width), bf16),
            pltpu.VMEM((n_head, width, sub), bf16),
            pltpu.VMEM((n_head, width, sub), bf16),
            pltpu.VMEM((n_patch, n_head, rows, width), bf16),
            pltpu.VMEM((n_patch, rows, sub), bf16),
            pltpu.VMEM((n_head, rows, sub), bf16),
            pltpu.VMEM((heads, rows, 1), jnp.float32),
            pltpu.VMEM((heads, rows, 1), jnp.float32),
            pltpu.VMEM((heads, rows, HEAD_DIM), jnp.float32),
            dma((2, 2, n_patch)),
            dma((2, n_patch)),
            dma((n_head,)),
            dma((n_head,)),
            dma((2, n_patch)),
            dma((n_head // CORES, n_patch)),
            dma((n_patch, n_head)),
            dma((n_patch, n_head)),
            dma((n_patch,)),
            dma((n_head,)),
        ],
        compiler_params=pltpu.CompilerParams(
            collective_id=0, has_side_effects=True, vmem_limit_bytes=40 * 1024 * 1024
        ),
    )(queries, fresh_keys, fresh_values, stale_keys, stale_values, out_weight)


def on_device(queries, fresh_keys, fresh_values, stale_keys, stale_values, out_weight, gate_scale):
    query_heads = head_view(queries)
    row_count = query_heads.shape[0]
    head_count = query_heads.shape[1]
    own_index = lax.axis_index("patch")
    own_start = own_index * row_count
    local = absorb(
        empty_state(row_count, head_count), block_scores(query_heads, fresh_keys), fresh_values
    )
    key_piece = lax.all_gather(stale_keys, "patch", axis=0, tiled=True)
    value_piece = lax.all_gather(stale_values, "patch", axis=0, tiled=True)
    key_count = key_piece.shape[0]
    key_step = 1024 if key_count > 1024 and key_count % 1024 == 0 else key_count

    def visit(block_index, inner):
        offset = block_index * key_step
        key_block = lax.dynamic_slice_in_dim(key_piece, offset, key_step, 0)
        value_block = lax.dynamic_slice_in_dim(value_piece, offset, key_step, 0)
        scores = block_scores(query_heads, key_block)
        position = offset + lax.iota(jnp.int32, key_step)
        own_rows = (position >= own_start) & (position < own_start + row_count)
        scores = jnp.where(own_rows[None, None, :], neg_large, scores)
        return absorb(inner, scores, value_block)

    run_max, run_total, run_acc = lax.fori_loop(0, key_count // key_step, visit, local)
    attended = (
        (run_acc / jnp.transpose(run_total)[:, :, None]).astype(jnp.bfloat16).reshape(row_count, -1)
    )
    partial_out = jnp.dot(
        attended,
        lax.all_gather(out_weight, "patch", axis=1, tiled=True),
        preferred_element_type=jnp.float32,
    )
    summed = lax.psum_scatter(partial_out, "head", scatter_dimension=1, tiled=True)
    return gate_scale[None, :] * summed


def solution(mesh):
    def fused(queries, fresh_keys, fresh_values, stale_keys, stale_values, out_weight, gate_scale):
        summed = fused_sublayer(
            n_patch, n_head, queries, fresh_keys, fresh_values, stale_keys, stale_values, out_weight
        )
        return gate_scale[None, :] * summed.astype(jnp.float32)

    n_patch, n_head = mesh.shape["patch"], mesh.shape["head"]
    square = n_patch == n_head and n_head % CORES == 0
    return jax.shard_map(
        fused if square else on_device,
        mesh=mesh,
        in_specs=(
            P(("groups", "patch"), "head"),
            P(("groups", "patch"), "head"),
            P(("groups", "patch"), "head"),
            P(("groups", "patch"), "head"),
            P(("groups", "patch"), "head"),
            P("head", "patch"),
            P(("groups", "head")),
        ),
        out_specs=P(("groups", "patch"), "head"),
        check_vma=False,
    )
```

```python
import functools

import jax
import jax.numpy as jnp
from jax import lax
from jax.experimental import pallas as pl
from jax.experimental.pallas import tpu as pltpu
from jax.sharding import PartitionSpec as P

HEAD_DIM = 128
MESH = pl.DeviceIdType.MESH
CORES = 2


neg_large = -1e30


def head_view(matrix):
    return matrix.reshape(matrix.shape[0], -1, HEAD_DIM)


def block_scores(query_heads, key_block):
    return jnp.einsum(
        "qhd,khd->hqk", query_heads, head_view(key_block), preferred_element_type=jnp.float32
    ) * HEAD_DIM ** (-0.5)


def absorb(running, scores, value_block):
    run_max, run_total, run_acc = running
    new_max = jnp.maximum(run_max, jnp.max(scores, axis=2))
    factor = jnp.exp(run_max - new_max)
    weights = jnp.exp(scores - new_max[:, :, None])
    new_total = run_total * factor + jnp.sum(weights, axis=2)
    mixture = jnp.einsum(
        "hqk,khd->qhd",
        weights.astype(jnp.bfloat16),
        head_view(value_block),
        preferred_element_type=jnp.float32,
    )
    new_acc = run_acc * jnp.transpose(factor)[:, :, None] + mixture
    return (new_max, new_total, new_acc)


def empty_state(row_count, head_count):
    return (
        jnp.full((head_count, row_count), neg_large, jnp.float32),
        jnp.zeros((head_count, row_count), jnp.float32),
        jnp.zeros((row_count, head_count, HEAD_DIM), jnp.float32),
    )


def sublayer_kernel(
    n_patch, n_head, q_hbm, fk_hbm, fv_hbm, sk_hbm, sv_hbm, w_hbm, out_ref,
    q_ref, fk_ref, fv_ref, w_ref,
    kbuf, vbuf, wsub, wbuf, abuf, ostage, obuf, top, total, acc,
    load, kv_send, kv_recv, w_send, w_recv, z_send, x_send, sib_send, a_recv, o_send, o_recv,
):
    g, p, h = lax.axis_index("groups"), lax.axis_index("patch"), lax.axis_index("head")
    core, chip = lax.rem(h, CORES), lax.div(h, CORES)
    sibling = h + 1 - 2 * core
    sub = wsub.shape[2]
    heads = q_ref.shape[1] // HEAD_DIM
    chips = n_head // CORES
    scale = HEAD_DIM ** (-0.5)

    def columns(i):
        return pl.ds(pl.multiple_of(i * HEAD_DIM, HEAD_DIM), HEAD_DIM)

    barrier = pltpu.get_barrier_semaphore()
    for s in range(n_patch):
        for j in range(n_head):
            @pl.when(jnp.logical_or(p != s, h != j))
            def _():
                pl.semaphore_signal(barrier, inc=1, device_id=(g, s, j), device_id_type=MESH)
    loads = [
        pltpu.make_async_copy(src, dst, load.at[k])
        for k, (src, dst) in enumerate(
            ((w_hbm, w_ref), (q_hbm, q_ref), (fk_hbm, fk_ref), (fv_hbm, fv_ref))
        )
    ]
    for copy in loads:
        copy.start()
    pl.semaphore_wait(barrier, n_patch * n_head - 1)

    def remote(src, dst, send, recv, patch, head):
        return pltpu.make_async_remote_copy(
            src_ref=src, dst_ref=dst, send_sem=send, recv_sem=recv,
            device_id=(g, patch, head), device_id_type=MESH,
        )

    def neighbour(side):
        return p + 1 - 2 * side

    def has_neighbour(side):
        return (p < n_patch - 1) if side == 0 else (p > 0)

    def slab_at(side, d):
        return p - d if side == 0 else p + d

    def is_slab(side, d):
        return (p - d >= 0) if side == 0 else jnp.logical_and(p + d < n_patch, d >= 1)

    def kv_copy(side, which, s, i, src):
        buf = (kbuf, vbuf)[which]
        return remote(
            src.at[:, columns(i)], buf.at[s, :, columns(i)], kv_send.at[side, which, s, i],
            kv_recv.at[which, s, i], neighbour(side), h,
        )

    def send_own(i):
        for which, src in ((0, sk_hbm), (1, sv_hbm)):
            for side in range(2):
                @pl.when(has_neighbour(side))
                def _():
                    kv_copy(side, which, p, i, src).start()

    send_own(0)

    def w_copy(j):
        return remote(wsub.at[j], wbuf.at[h], w_send.at[j], w_recv.at[h], p, j)

    loads[0].wait()
    for j in range(n_head):
        wsub[j] = w_ref[:, j * sub:(j + 1) * sub]

        @pl.when(h != j)
        def _():
            w_copy(j).start()
    wbuf[h] = wsub[h]
    for copy in loads[1:]:
        copy.wait()

    def absorb_block(i, keys, values, first):
        scores = lax.dot_general(
            q_ref[:, columns(i)], keys, (((1,), (1,)), ((), ())),
            preferred_element_type=jnp.float32,
        )
        new_top = jnp.max(scores, axis=1, keepdims=True)
        if not first:
            old_top = top[...]
            new_top = jnp.maximum(old_top, new_top)
            factor = jnp.exp((old_top - new_top) * scale)
        weights = jnp.exp((scores - new_top) * scale)
        new_total = jnp.sum(weights, axis=1, keepdims=True)
        mixture = jnp.dot(weights.astype(jnp.bfloat16), values, preferred_element_type=jnp.float32)
        if not first:
            new_total = new_total + total[...] * factor
            mixture = mixture + acc[...] * factor
        top[...] = new_top
        total[...] = new_total
        acc[...] = mixture

    def kv_step(i, d):
        for which in range(2):
            for side in range(2):
                s = slab_at(side, d)

                @pl.when(is_slab(side, d))
                def _():
                    copy = kv_copy(side, which, s, i, (kbuf, vbuf)[which].at[s])
                    copy.wait_recv()

                    @pl.when(has_neighbour(side))
                    def _():
                        copy.start()

        @pl.when(jnp.logical_and(d == 1, i + 1 < heads))
        def _():
            send_own(i + 1)
        for side in range(2):
            s = slab_at(side, d)

            @pl.when(is_slab(side, d))
            def _():
                absorb_block(i, kbuf[s, :, columns(i)], vbuf[s, :, columns(i)], False)

    def piece(s, head, i):
        return abuf.at[s, head, :, columns(i)]

    def z_copy(side, s, i):
        return remote(
            piece(s, h, i), piece(s, h, i), z_send.at[side, s, i], a_recv.at[s, h, i],
            neighbour(side), h,
        )

    def x_copy(xx, s, i):
        return remote(
            piece(s, h, i), piece(s, h, i), x_send.at[xx, s, i], a_recv.at[s, h, i],
            p, xx * CORES + core,
        )

    def sib_copy(s, head, i):
        return remote(
            piece(s, head, i), piece(s, head, i), sib_send.at[s, head, i], a_recv.at[s, head, i],
            p, sibling,
        )

    def spread(s, i):
        for xx in range(chips):
            @pl.when(chip != xx)
            def _():
                x_copy(xx, s, i).start()
        sib_copy(s, h, i).start()

    def o_copy(s):
        return remote(ostage.at[s], obuf.at[h], o_send.at[s], o_recv.at[h], s, p)

    def stays(s):
        return jnp.logical_and(s == p, h == p)

    def project(s):
        for i in range(heads):
            for xx in range(chips):
                head = xx * CORES + 1 - core
                remote(
                    piece(s, head, i), piece(s, head, i), sib_send.at[s, h, i],
                    a_recv.at[s, head, i], p, sibling,
                ).wait_recv()
        term = jnp.dot(abuf[s, 0], wbuf[0], preferred_element_type=jnp.float32)
        for j in range(1, n_head):
            term = term + jnp.dot(abuf[s, j], wbuf[j], preferred_element_type=jnp.float32)
        ostage[s] = term.astype(jnp.bfloat16)

        @pl.when(stays(s))
        def _():
            obuf[h] = ostage[s]

        @pl.when(jnp.logical_not(stays(s)))
        def _():
            o_copy(s).start()

    def spread_step(i, d):
        for side in range(2):
            s = slab_at(side, d)

            @pl.when(is_slab(side, d))
            def _():
                copy = z_copy(side, s, i)
                copy.wait_recv()

                @pl.when(has_neighbour(side))
                def _():
                    copy.start()
                spread(s, i)
        for side in range(2):
            s = slab_at(side, d - 1)

            @pl.when(is_slab(side, d - 1))
            def _():
                for xx in range(chips):
                    @pl.when(chip != xx)
                    def _():
                        head = xx * CORES + core
                        remote(
                            piece(s, head, i), piece(s, head, i), x_send.at[xx, s, i],
                            a_recv.at[s, head, i], p, head,
                        ).wait_recv()
                        sib_copy(s, head, i).start()

    def head_step(i, carry):
        @pl.when(i < heads)
        def _():
            absorb_block(i, fk_ref[:, columns(i)], fv_ref[:, columns(i)], True)

        @pl.when(i == heads)
        def _():
            for j in range(n_head):
                @pl.when(h != j)
                def _():
                    remote(wsub.at[j], wbuf.at[j], w_send.at[j], w_recv.at[j], p, j).wait_recv()

        def hop(d, inner):
            @pl.when(jnp.logical_and(i < heads, d < n_patch))
            def _():
                kv_step(i, d)

            @pl.when(i >= 1)
            def _():
                spread_step(i - 1, d)

            @pl.when(i == heads)
            def _():
                for side in range(2):
                    @pl.when(is_slab(side, d - 1))
                    def _():
                        project(slab_at(side, d - 1))
            return inner

        lax.fori_loop(1, n_patch + 1, hop, 0)

        @pl.when(i < heads)
        def _():
            abuf[p, h, :, columns(i)] = (acc[...] / total[...]).astype(jnp.bfloat16)
            for side in range(2):
                @pl.when(has_neighbour(side))
                def _():
                    z_copy(side, p, i).start()
            spread(p, i)
        return carry

    lax.fori_loop(0, heads + 1, head_step, 0)

    for j in range(n_head):
        @pl.when(jnp.logical_or(p != h, h != j))
        def _():
            remote(ostage.at[0], obuf.at[j], o_send.at[0], o_recv.at[j], h, j).wait_recv()
        out_ref[:, j * sub:(j + 1) * sub] = obuf[j]

    for j in range(n_head):
        @pl.when(h != j)
        def _():
            w_copy(j).wait_send()

    def drain(s, carry):
        def drain_head(i, inner):
            for side in range(2):
                passes = (s <= p) if side == 0 else (s >= p)

                @pl.when(jnp.logical_and(passes, has_neighbour(side)))
                def _():
                    kv_copy(side, 0, s, i, kbuf.at[s]).wait_send()
                    kv_copy(side, 1, s, i, vbuf.at[s]).wait_send()
                    z_copy(side, s, i).wait_send()
            for xx in range(chips):
                @pl.when(chip != xx)
                def _():
                    x_copy(xx, s, i).wait_send()
                sib_copy(s, xx * CORES + core, i).wait_send()
            return inner

        lax.fori_loop(0, heads, drain_head, 0)

        @pl.when(jnp.logical_not(stays(s)))
        def _():
            o_copy(s).wait_send()
        return carry

    lax.fori_loop(0, n_patch, drain, 0)


def fused_sublayer(n_patch, n_head, queries, fresh_keys, fresh_values, stale_keys, stale_values, out_weight):
    rows, width = queries.shape
    columns = out_weight.shape[1]
    sub = columns // n_head
    heads = width // HEAD_DIM
    bf16, dma = jnp.bfloat16, pltpu.SemaphoreType.DMA
    return pl.pallas_call(
        functools.partial(sublayer_kernel, n_patch, n_head),
        out_shape=jax.ShapeDtypeStruct((rows, columns), bf16),
        in_specs=[pl.BlockSpec(memory_space=pl.ANY)] * 6,
        out_specs=pl.BlockSpec(memory_space=pltpu.VMEM),
        scratch_shapes=[
            pltpu.VMEM((rows, width), bf16),
            pltpu.VMEM((rows, width), bf16),
            pltpu.VMEM((rows, width), bf16),
            pltpu.VMEM((width, columns), bf16),
            pltpu.VMEM((n_patch, rows, width), bf16),
            pltpu.VMEM((n_patch, rows, width), bf16),
            pltpu.VMEM((n_head, width, sub), bf16),
            pltpu.VMEM((n_head, width, sub), bf16),
            pltpu.VMEM((n_patch, n_head, rows, width), bf16),
            pltpu.VMEM((n_patch, rows, sub), bf16),
            pltpu.VMEM((n_head, rows, sub), bf16),
            pltpu.VMEM((rows, 1), jnp.float32),
            pltpu.VMEM((rows, 1), jnp.float32),
            pltpu.VMEM((rows, HEAD_DIM), jnp.float32),
            dma((4,)),
            dma((2, 2, n_patch, heads)),
            dma((2, n_patch, heads)),
            dma((n_head,)),
            dma((n_head,)),
            dma((2, n_patch, heads)),
            dma((n_head // CORES, n_patch, heads)),
            dma((n_patch, n_head, heads)),
            dma((n_patch, n_head, heads)),
            dma((n_patch,)),
            dma((n_head,)),
        ],
        compiler_params=pltpu.CompilerParams(
            collective_id=0, has_side_effects=True, vmem_limit_bytes=56 * 1024 * 1024
        ),
    )(queries, fresh_keys, fresh_values, stale_keys, stale_values, out_weight)


def on_device(queries, fresh_keys, fresh_values, stale_keys, stale_values, out_weight, gate_scale):
    query_heads = head_view(queries)
    row_count = query_heads.shape[0]
    head_count = query_heads.shape[1]
    own_index = lax.axis_index("patch")
    own_start = own_index * row_count
    local = absorb(
        empty_state(row_count, head_count), block_scores(query_heads, fresh_keys), fresh_values
    )
    key_piece = lax.all_gather(stale_keys, "patch", axis=0, tiled=True)
    value_piece = lax.all_gather(stale_values, "patch", axis=0, tiled=True)
    key_count = key_piece.shape[0]
    key_step = 1024 if key_count > 1024 and key_count % 1024 == 0 else key_count

    def visit(block_index, inner):
        offset = block_index * key_step
        key_block = lax.dynamic_slice_in_dim(key_piece, offset, key_step, 0)
        value_block = lax.dynamic_slice_in_dim(value_piece, offset, key_step, 0)
        scores = block_scores(query_heads, key_block)
        position = offset + lax.iota(jnp.int32, key_step)
        own_rows = (position >= own_start) & (position < own_start + row_count)
        scores = jnp.where(own_rows[None, None, :], neg_large, scores)
        return absorb(inner, scores, value_block)

    run_max, run_total, run_acc = lax.fori_loop(0, key_count // key_step, visit, local)
    attended = (
        (run_acc / jnp.transpose(run_total)[:, :, None]).astype(jnp.bfloat16).reshape(row_count, -1)
    )
    partial_out = jnp.dot(
        attended,
        lax.all_gather(out_weight, "patch", axis=1, tiled=True),
        preferred_element_type=jnp.float32,
    )
    summed = lax.psum_scatter(partial_out, "head", scatter_dimension=1, tiled=True)
    return gate_scale[None, :] * summed


def solution(mesh):
    def fused(queries, fresh_keys, fresh_values, stale_keys, stale_values, out_weight, gate_scale):
        summed = fused_sublayer(
            n_patch, n_head, queries, fresh_keys, fresh_values, stale_keys, stale_values, out_weight
        )
        return gate_scale[None, :] * summed.astype(jnp.float32)

    n_patch, n_head = mesh.shape["patch"], mesh.shape["head"]
    square = n_patch == n_head and n_head % CORES == 0
    return jax.shard_map(
        fused if square else on_device,
        mesh=mesh,
        in_specs=(
            P(("groups", "patch"), "head"),
            P(("groups", "patch"), "head"),
            P(("groups", "patch"), "head"),
            P(("groups", "patch"), "head"),
            P(("groups", "patch"), "head"),
            P("head", "patch"),
            P(("groups", "head")),
        ),
        out_specs=P(("groups", "patch"), "head"),
        check_vma=False,
    )
```

```python
import functools

import jax
import jax.numpy as jnp
from jax import lax
from jax.experimental import pallas as pl
from jax.experimental.pallas import tpu as pltpu
from jax.sharding import PartitionSpec as P

HEAD_DIM = 128
MESH = pl.DeviceIdType.MESH
CORES = 2


neg_large = -1e30


def head_view(matrix):
    return matrix.reshape(matrix.shape[0], -1, HEAD_DIM)


def block_scores(query_heads, key_block):
    return jnp.einsum(
        "qhd,khd->hqk", query_heads, head_view(key_block), preferred_element_type=jnp.float32
    ) * HEAD_DIM ** (-0.5)


def absorb(running, scores, value_block):
    run_max, run_total, run_acc = running
    new_max = jnp.maximum(run_max, jnp.max(scores, axis=2))
    factor = jnp.exp(run_max - new_max)
    weights = jnp.exp(scores - new_max[:, :, None])
    new_total = run_total * factor + jnp.sum(weights, axis=2)
    mixture = jnp.einsum(
        "hqk,khd->qhd",
        weights.astype(jnp.bfloat16),
        head_view(value_block),
        preferred_element_type=jnp.float32,
    )
    new_acc = run_acc * jnp.transpose(factor)[:, :, None] + mixture
    return (new_max, new_total, new_acc)


def empty_state(row_count, head_count):
    return (
        jnp.full((head_count, row_count), neg_large, jnp.float32),
        jnp.zeros((head_count, row_count), jnp.float32),
        jnp.zeros((row_count, head_count, HEAD_DIM), jnp.float32),
    )


def sublayer_kernel(
    n_patch, n_head, q_hbm, fk_hbm, fv_hbm, sk_hbm, sv_hbm, w_hbm, out_ref,
    q_ref, fk_ref, fv_ref, w_ref, kbuf, vbuf, wsub, wbuf, abuf, ostage, obuf, top, total, acc,
    load, kv_send, kv_recv, w_send, w_recv, z_send, x_send, sib_send, a_recv, o_send, o_recv,
):
    g, p, h = lax.axis_index("groups"), lax.axis_index("patch"), lax.axis_index("head")
    core, chip = lax.rem(h, CORES), lax.div(h, CORES)
    sibling = h + 1 - 2 * core
    sub = wsub.shape[2]
    heads = q_ref.shape[1] // HEAD_DIM
    scale = HEAD_DIM ** (-0.5)

    barrier = pltpu.get_barrier_semaphore()
    for s in range(n_patch):
        for j in range(n_head):
            @pl.when(jnp.logical_or(p != s, h != j))
            def _():
                pl.semaphore_signal(barrier, inc=1, device_id=(g, s, j), device_id_type=MESH)
    loads = [
        pltpu.make_async_copy(src, dst, load.at[k])
        for k, (src, dst) in enumerate(
            ((w_hbm, w_ref), (q_hbm, q_ref), (fk_hbm, fk_ref), (fv_hbm, fv_ref))
        )
    ]
    for copy in loads:
        copy.start()
    pl.semaphore_wait(barrier, n_patch * n_head - 1)

    def remote(src, dst, send, recv, patch, head):
        return pltpu.make_async_remote_copy(
            src_ref=src, dst_ref=dst, send_sem=send, recv_sem=recv,
            device_id=(g, patch, head), device_id_type=MESH,
        )

    def neighbour(side):
        return p + 1 - 2 * side

    def has_neighbour(side):
        return (p < n_patch - 1) if side == 0 else (p > 0)

    def slab_at(side, d):
        return p - d if side == 0 else p + d

    def is_slab(side, d):
        return (p - d >= 0) if side == 0 else jnp.logical_and(p + d < n_patch, d >= 1)

    def kv_copy(side, which, s, src):
        buf = (kbuf, vbuf)[which]
        return remote(
            src, buf.at[s], kv_send.at[side, which, s], kv_recv.at[which, s], neighbour(side), h
        )

    for which, src in ((0, sk_hbm), (1, sv_hbm)):
        for side in range(2):
            @pl.when(has_neighbour(side))
            def _():
                kv_copy(side, which, p, src).start()

    def w_copy(j):
        return remote(wsub.at[j], wbuf.at[h], w_send.at[j], w_recv.at[h], p, j)

    loads[0].wait()
    for j in range(n_head):
        wsub[j] = w_ref[:, j * sub:(j + 1) * sub]

        @pl.when(h != j)
        def _():
            w_copy(j).start()
    wbuf[h] = wsub[h]
    for copy in loads[1:]:
        copy.wait()

    def absorb_block(keys, values, first):
        for i in range(heads):
            cols = slice(i * HEAD_DIM, (i + 1) * HEAD_DIM)
            scores = lax.dot_general(
                q_ref[:, cols], keys[:, cols], (((1,), (1,)), ((), ())),
                preferred_element_type=jnp.float32,
            )
            new_top = jnp.max(scores, axis=1, keepdims=True)
            if not first:
                old_top = top[i]
                new_top = jnp.maximum(old_top, new_top)
                factor = jnp.exp((old_top - new_top) * scale)
            weights = jnp.exp((scores - new_top) * scale)
            new_total = jnp.sum(weights, axis=1, keepdims=True)
            mixture = jnp.dot(
                weights.astype(jnp.bfloat16), values[:, cols], preferred_element_type=jnp.float32
            )
            if not first:
                new_total = new_total + total[i] * factor
                mixture = mixture + acc[i] * factor
            top[i] = new_top
            total[i] = new_total
            acc[i] = mixture

    absorb_block(fk_ref[...], fv_ref[...], True)

    def kv_step(d, carry):
        for which in range(2):
            for side in range(2):
                s = slab_at(side, d)

                @pl.when(is_slab(side, d))
                def _():
                    buf = (kbuf, vbuf)[which]
                    copy = kv_copy(side, which, s, buf.at[s])
                    copy.wait_recv()

                    @pl.when(has_neighbour(side))
                    def _():
                        copy.start()
        for side in range(2):
            s = slab_at(side, d)

            @pl.when(is_slab(side, d))
            def _():
                absorb_block(kbuf.at[s][...], vbuf.at[s][...], False)
        return carry

    lax.fori_loop(1, n_patch, kv_step, 0)

    for i in range(heads):
        abuf[p, h, :, i * HEAD_DIM:(i + 1) * HEAD_DIM] = (acc[i] / total[i]).astype(jnp.bfloat16)

    def z_copy(s):
        return remote(abuf.at[p, h], abuf.at[p, h], z_send.at[s], a_recv.at[p, h], s, h)

    def z_arrival(s):
        return remote(abuf.at[s, h], abuf.at[s, h], z_send.at[s], a_recv.at[s, h], s, h)

    def x_copy(xx, s):
        return remote(
            abuf.at[s, h], abuf.at[s, h], x_send.at[xx, s], a_recv.at[s, h], p, xx * CORES + core
        )

    def sib_copy(s, head):
        return remote(
            abuf.at[s, head], abuf.at[s, head], sib_send.at[s, head], a_recv.at[s, head], p, sibling
        )

    def spread(s):
        for xx in range(n_head // CORES):
            @pl.when(chip != xx)
            def _():
                x_copy(xx, s).start()
        sib_copy(s, h).start()

    spread(p)
    for d in range(1, n_patch):
        for side in range(2):
            @pl.when(is_slab(side, d))
            def _():
                z_copy(slab_at(side, d)).start()

    for j in range(n_head):
        @pl.when(h != j)
        def _():
            remote(wsub.at[j], wbuf.at[j], w_send.at[j], w_recv.at[j], p, j).wait_recv()

    def o_copy(s):
        return remote(ostage.at[s], obuf.at[h], o_send.at[s], o_recv.at[h], s, p)

    def stays(s):
        return jnp.logical_and(s == p, h == p)

    def project(s):
        for xx in range(n_head // CORES):
            head = xx * CORES + 1 - core
            sib_in = remote(
                abuf.at[s, head], abuf.at[s, head], sib_send.at[s, h], a_recv.at[s, head], p, sibling
            )
            sib_in.wait_recv()
        term = jnp.dot(abuf[s, 0], wbuf[0], preferred_element_type=jnp.float32)
        for j in range(1, n_head):
            term = term + jnp.dot(abuf[s, j], wbuf[j], preferred_element_type=jnp.float32)
        ostage[s] = term.astype(jnp.bfloat16)

        @pl.when(stays(s))
        def _():
            obuf[h] = ostage[s]

        @pl.when(jnp.logical_not(stays(s)))
        def _():
            o_copy(s).start()

    def spread_step(d, carry):
        for side in range(2):
            s = slab_at(side, d)

            @pl.when(is_slab(side, d))
            def _():
                z_arrival(s).wait_recv()
                spread(s)
        for side in range(2):
            s = slab_at(side, d - 1)

            @pl.when(is_slab(side, d - 1))
            def _():
                for xx in range(n_head // CORES):
                    @pl.when(chip != xx)
                    def _():
                        head = xx * CORES + core
                        remote(
                            abuf.at[s, head], abuf.at[s, head], x_send.at[xx, s],
                            a_recv.at[s, head], p, head,
                        ).wait_recv()
                        sib_copy(s, head).start()
        for side in range(2):
            s = slab_at(side, d - 1)

            @pl.when(is_slab(side, d - 1))
            def _():
                project(s)
        return carry

    lax.fori_loop(1, n_patch + 1, spread_step, 0)

    for j in range(n_head):
        @pl.when(jnp.logical_or(p != h, h != j))
        def _():
            remote(ostage.at[0], obuf.at[j], o_send.at[0], o_recv.at[j], h, j).wait_recv()
        out_ref[:, j * sub:(j + 1) * sub] = obuf[j]

    for j in range(n_head):
        @pl.when(h != j)
        def _():
            w_copy(j).wait_send()

    def drain(s, carry):
        for side in range(2):
            passes = (s <= p) if side == 0 else (s >= p)

            @pl.when(jnp.logical_and(passes, has_neighbour(side)))
            def _():
                kv_copy(side, 0, s, kbuf.at[s]).wait_send()
                kv_copy(side, 1, s, vbuf.at[s]).wait_send()

        @pl.when(s != p)
        def _():
            z_copy(s).wait_send()
        for xx in range(n_head // CORES):
            @pl.when(chip != xx)
            def _():
                x_copy(xx, s).wait_send()
            sib_copy(s, xx * CORES + core).wait_send()

        @pl.when(jnp.logical_not(stays(s)))
        def _():
            o_copy(s).wait_send()
        return carry

    lax.fori_loop(0, n_patch, drain, 0)


def fused_sublayer(n_patch, n_head, queries, fresh_keys, fresh_values, stale_keys, stale_values, out_weight):
    rows, width = queries.shape
    columns = out_weight.shape[1]
    sub = columns // n_head
    heads = width // HEAD_DIM
    bf16, dma = jnp.bfloat16, pltpu.SemaphoreType.DMA
    return pl.pallas_call(
        functools.partial(sublayer_kernel, n_patch, n_head),
        out_shape=jax.ShapeDtypeStruct((rows, columns), bf16),
        in_specs=[pl.BlockSpec(memory_space=pl.ANY)] * 6,
        out_specs=pl.BlockSpec(memory_space=pltpu.VMEM),
        scratch_shapes=[
            pltpu.VMEM((rows, width), bf16),
            pltpu.VMEM((rows, width), bf16),
            pltpu.VMEM((rows, width), bf16),
            pltpu.VMEM((width, columns), bf16),
            pltpu.VMEM((n_patch, rows, width), bf16),
            pltpu.VMEM((n_patch, rows, width), bf16),
            pltpu.VMEM((n_head, width, sub), bf16),
            pltpu.VMEM((n_head, width, sub), bf16),
            pltpu.VMEM((n_patch, n_head, rows, width), bf16),
            pltpu.VMEM((n_patch, rows, sub), bf16),
            pltpu.VMEM((n_head, rows, sub), bf16),
            pltpu.VMEM((heads, rows, 1), jnp.float32),
            pltpu.VMEM((heads, rows, 1), jnp.float32),
            pltpu.VMEM((heads, rows, HEAD_DIM), jnp.float32),
            dma((4,)),
            dma((2, 2, n_patch)),
            dma((2, n_patch)),
            dma((n_head,)),
            dma((n_head,)),
            dma((n_patch,)),
            dma((n_head // CORES, n_patch)),
            dma((n_patch, n_head)),
            dma((n_patch, n_head)),
            dma((n_patch,)),
            dma((n_head,)),
        ],
        compiler_params=pltpu.CompilerParams(
            collective_id=0, has_side_effects=True, vmem_limit_bytes=56 * 1024 * 1024
        ),
    )(queries, fresh_keys, fresh_values, stale_keys, stale_values, out_weight)


def on_device(queries, fresh_keys, fresh_values, stale_keys, stale_values, out_weight, gate_scale):
    query_heads = head_view(queries)
    row_count = query_heads.shape[0]
    head_count = query_heads.shape[1]
    own_index = lax.axis_index("patch")
    own_start = own_index * row_count
    local = absorb(
        empty_state(row_count, head_count), block_scores(query_heads, fresh_keys), fresh_values
    )
    key_piece = lax.all_gather(stale_keys, "patch", axis=0, tiled=True)
    value_piece = lax.all_gather(stale_values, "patch", axis=0, tiled=True)
    key_count = key_piece.shape[0]
    key_step = 1024 if key_count > 1024 and key_count % 1024 == 0 else key_count

    def visit(block_index, inner):
        offset = block_index * key_step
        key_block = lax.dynamic_slice_in_dim(key_piece, offset, key_step, 0)
        value_block = lax.dynamic_slice_in_dim(value_piece, offset, key_step, 0)
        scores = block_scores(query_heads, key_block)
        position = offset + lax.iota(jnp.int32, key_step)
        own_rows = (position >= own_start) & (position < own_start + row_count)
        scores = jnp.where(own_rows[None, None, :], neg_large, scores)
        return absorb(inner, scores, value_block)

    run_max, run_total, run_acc = lax.fori_loop(0, key_count // key_step, visit, local)
    attended = (
        (run_acc / jnp.transpose(run_total)[:, :, None]).astype(jnp.bfloat16).reshape(row_count, -1)
    )
    partial_out = jnp.dot(
        attended,
        lax.all_gather(out_weight, "patch", axis=1, tiled=True),
        preferred_element_type=jnp.float32,
    )
    summed = lax.psum_scatter(partial_out, "head", scatter_dimension=1, tiled=True)
    return gate_scale[None, :] * summed


def solution(mesh):
    def fused(queries, fresh_keys, fresh_values, stale_keys, stale_values, out_weight, gate_scale):
        summed = fused_sublayer(
            n_patch, n_head, queries, fresh_keys, fresh_values, stale_keys, stale_values, out_weight
        )
        return gate_scale[None, :] * summed.astype(jnp.float32)

    n_patch, n_head = mesh.shape["patch"], mesh.shape["head"]
    square = n_patch == n_head and n_head % CORES == 0
    return jax.shard_map(
        fused if square else on_device,
        mesh=mesh,
        in_specs=(
            P(("groups", "patch"), "head"),
            P(("groups", "patch"), "head"),
            P(("groups", "patch"), "head"),
            P(("groups", "patch"), "head"),
            P(("groups", "patch"), "head"),
            P("head", "patch"),
            P(("groups", "head")),
        ),
        out_specs=P(("groups", "patch"), "head"),
        check_vma=False,
    )
```

```python
import functools

import jax
import jax.numpy as jnp
from jax import lax
from jax.experimental import pallas as pl
from jax.experimental.pallas import tpu as pltpu
from jax.sharding import PartitionSpec as P

HEAD_DIM = 128
MESH = pl.DeviceIdType.MESH
CORES = 2


neg_large = -1e30


def head_view(matrix):
    return matrix.reshape(matrix.shape[0], -1, HEAD_DIM)


def block_scores(query_heads, key_block):
    return jnp.einsum(
        "qhd,khd->hqk", query_heads, head_view(key_block), preferred_element_type=jnp.float32
    ) * HEAD_DIM ** (-0.5)


def absorb(running, scores, value_block):
    run_max, run_total, run_acc = running
    new_max = jnp.maximum(run_max, jnp.max(scores, axis=2))
    factor = jnp.exp(run_max - new_max)
    weights = jnp.exp(scores - new_max[:, :, None])
    new_total = run_total * factor + jnp.sum(weights, axis=2)
    mixture = jnp.einsum(
        "hqk,khd->qhd",
        weights.astype(jnp.bfloat16),
        head_view(value_block),
        preferred_element_type=jnp.float32,
    )
    new_acc = run_acc * jnp.transpose(factor)[:, :, None] + mixture
    return (new_max, new_total, new_acc)


def empty_state(row_count, head_count):
    return (
        jnp.full((head_count, row_count), neg_large, jnp.float32),
        jnp.zeros((head_count, row_count), jnp.float32),
        jnp.zeros((row_count, head_count, HEAD_DIM), jnp.float32),
    )


def sublayer_kernel(
    n_patch, n_head, q_hbm, fk_hbm, fv_hbm, sk_hbm, sv_hbm, w_hbm, out_ref,
    q_ref, fk_ref, fv_ref, sk_ref, sv_ref, w_ref,
    kbuf, vbuf, wsub, wbuf, abuf, ostage, obuf, top, total, acc,
    load, kv_send, kv_recv, w_send, w_recv, z_send, x_send, sib_send, a_recv, o_send, o_recv,
):
    g, p, h = lax.axis_index("groups"), lax.axis_index("patch"), lax.axis_index("head")
    core, chip = lax.rem(h, CORES), lax.div(h, CORES)
    sibling = h + 1 - 2 * core
    sub = wsub.shape[2]
    heads = q_ref.shape[1] // HEAD_DIM
    chips = n_head // CORES
    scale = HEAD_DIM ** (-0.5)

    def columns(i):
        return pl.ds(pl.multiple_of(i * HEAD_DIM, HEAD_DIM), HEAD_DIM)

    barrier = pltpu.get_barrier_semaphore()
    for s in range(n_patch):
        for j in range(n_head):
            @pl.when(jnp.logical_or(p != s, h != j))
            def _():
                pl.semaphore_signal(barrier, inc=1, device_id=(g, s, j), device_id_type=MESH)
    pairs = [
        (src.at[:, i * HEAD_DIM:(i + 1) * HEAD_DIM], dst.at[i])
        for i in range(heads) for src, dst in ((sk_hbm, sk_ref), (sv_hbm, sv_ref))
    ]
    pairs += [(w_hbm, w_ref), (q_hbm, q_ref), (fk_hbm, fk_ref), (fv_hbm, fv_ref)]
    loads = [
        pltpu.make_async_copy(src, dst, load.at[k]) for k, (src, dst) in enumerate(pairs)
    ]
    for copy in loads:
        copy.start()
    for copy in loads[:2 * heads]:
        copy.wait()
    loads = loads[2 * heads:]
    pl.semaphore_wait(barrier, n_patch * n_head - 1)

    def remote(src, dst, send, recv, patch, head):
        return pltpu.make_async_remote_copy(
            src_ref=src, dst_ref=dst, send_sem=send, recv_sem=recv,
            device_id=(g, patch, head), device_id_type=MESH,
        )

    def neighbour(side):
        return p + 1 - 2 * side

    def has_neighbour(side):
        return (p < n_patch - 1) if side == 0 else (p > 0)

    def slab_at(side, d):
        return p - d if side == 0 else p + d

    def is_slab(side, d):
        return (p - d >= 0) if side == 0 else jnp.logical_and(p + d < n_patch, d >= 1)

    def kv_copy(side, which, s, i, src):
        buf = (kbuf, vbuf)[which]
        return remote(
            src.at[i], buf.at[s, i], kv_send.at[side, which, s, i],
            kv_recv.at[which, s, i], neighbour(side), h,
        )

    def send_own(i):
        for which, src in ((0, sk_ref), (1, sv_ref)):
            for side in range(2):
                @pl.when(has_neighbour(side))
                def _():
                    kv_copy(side, which, p, i, src).start()

    send_own(0)

    def w_copy(j):
        return remote(wsub.at[j], wbuf.at[h], w_send.at[j], w_recv.at[h], p, j)

    loads[0].wait()
    for j in range(n_head):
        wsub[j] = w_ref[:, j * sub:(j + 1) * sub]

        @pl.when(h != j)
        def _():
            w_copy(j).start()
    wbuf[h] = wsub[h]
    for copy in loads[1:]:
        copy.wait()

    def absorb_block(i, keys, values, first):
        scores = lax.dot_general(
            q_ref[:, columns(i)], keys, (((1,), (1,)), ((), ())),
            preferred_element_type=jnp.float32,
        )
        new_top = jnp.max(scores, axis=1, keepdims=True)
        if not first:
            old_top = top[...]
            new_top = jnp.maximum(old_top, new_top)
            factor = jnp.exp((old_top - new_top) * scale)
        weights = jnp.exp((scores - new_top) * scale)
        new_total = jnp.sum(weights, axis=1, keepdims=True)
        mixture = jnp.dot(weights.astype(jnp.bfloat16), values, preferred_element_type=jnp.float32)
        if not first:
            new_total = new_total + total[...] * factor
            mixture = mixture + acc[...] * factor
        top[...] = new_top
        total[...] = new_total
        acc[...] = mixture

    def kv_step(i, d):
        for which in range(2):
            for side in range(2):
                s = slab_at(side, d)

                @pl.when(is_slab(side, d))
                def _():
                    copy = kv_copy(side, which, s, i, (kbuf, vbuf)[which].at[s])
                    copy.wait_recv()

                    @pl.when(has_neighbour(side))
                    def _():
                        copy.start()

        @pl.when(jnp.logical_and(d == 1, i + 1 < heads))
        def _():
            send_own(i + 1)
        for side in range(2):
            s = slab_at(side, d)

            @pl.when(is_slab(side, d))
            def _():
                absorb_block(i, kbuf[s, i], vbuf[s, i], False)

    def piece(s, head, i):
        return abuf.at[s, head, i]

    def z_copy(side, s, i):
        return remote(
            piece(s, h, i), piece(s, h, i), z_send.at[side, s, i], a_recv.at[s, h, i],
            neighbour(side), h,
        )

    def x_copy(xx, s, i):
        return remote(
            piece(s, h, i), piece(s, h, i), x_send.at[xx, s, i], a_recv.at[s, h, i],
            p, xx * CORES + core,
        )

    def sib_copy(s, head, i):
        return remote(
            piece(s, head, i), piece(s, head, i), sib_send.at[s, head, i], a_recv.at[s, head, i],
            p, sibling,
        )

    def spread(s, i):
        for xx in range(chips):
            @pl.when(chip != xx)
            def _():
                x_copy(xx, s, i).start()
        sib_copy(s, h, i).start()

    def o_copy(s):
        return remote(ostage.at[s], obuf.at[h], o_send.at[s], o_recv.at[h], s, p)

    def stays(s):
        return jnp.logical_and(s == p, h == p)

    def project(s):
        for i in range(heads):
            for xx in range(chips):
                head = xx * CORES + 1 - core
                remote(
                    piece(s, head, i), piece(s, head, i), sib_send.at[s, h, i],
                    a_recv.at[s, head, i], p, sibling,
                ).wait_recv()
        term = 0.0
        for j in range(n_head):
            group = jnp.concatenate([abuf[s, j, i] for i in range(heads)], axis=1)
            term = term + jnp.dot(group, wbuf[j], preferred_element_type=jnp.float32)
        ostage[s] = term.astype(jnp.bfloat16)

        @pl.when(stays(s))
        def _():
            obuf[h] = ostage[s]

        @pl.when(jnp.logical_not(stays(s)))
        def _():
            o_copy(s).start()

    def spread_step(i, d):
        for side in range(2):
            s = slab_at(side, d)

            @pl.when(is_slab(side, d))
            def _():
                copy = z_copy(side, s, i)
                copy.wait_recv()

                @pl.when(has_neighbour(side))
                def _():
                    copy.start()
                spread(s, i)
        for side in range(2):
            s = slab_at(side, d - 1)

            @pl.when(is_slab(side, d - 1))
            def _():
                for xx in range(chips):
                    @pl.when(chip != xx)
                    def _():
                        head = xx * CORES + core
                        remote(
                            piece(s, head, i), piece(s, head, i), x_send.at[xx, s, i],
                            a_recv.at[s, head, i], p, head,
                        ).wait_recv()
                        sib_copy(s, head, i).start()

    def head_step(i, carry):
        @pl.when(i < heads)
        def _():
            absorb_block(i, fk_ref[:, columns(i)], fv_ref[:, columns(i)], True)

        @pl.when(i == heads)
        def _():
            for j in range(n_head):
                @pl.when(h != j)
                def _():
                    remote(wsub.at[j], wbuf.at[j], w_send.at[j], w_recv.at[j], p, j).wait_recv()

        def hop(d, inner):
            @pl.when(jnp.logical_and(i < heads, d < n_patch))
            def _():
                kv_step(i, d)

            @pl.when(i >= 1)
            def _():
                spread_step(i - 1, d)

            @pl.when(i == heads)
            def _():
                for side in range(2):
                    @pl.when(is_slab(side, d - 1))
                    def _():
                        project(slab_at(side, d - 1))
            return inner

        lax.fori_loop(1, n_patch + 1, hop, 0)

        @pl.when(i < heads)
        def _():
            abuf[p, h, i] = (acc[...] / total[...]).astype(jnp.bfloat16)
            for side in range(2):
                @pl.when(has_neighbour(side))
                def _():
                    z_copy(side, p, i).start()
            spread(p, i)
        return carry

    lax.fori_loop(0, heads + 1, head_step, 0)

    for j in range(n_head):
        @pl.when(jnp.logical_or(p != h, h != j))
        def _():
            remote(ostage.at[0], obuf.at[j], o_send.at[0], o_recv.at[j], h, j).wait_recv()
        out_ref[:, j * sub:(j + 1) * sub] = obuf[j]

    for j in range(n_head):
        @pl.when(h != j)
        def _():
            w_copy(j).wait_send()

    def drain(s, carry):
        def drain_head(i, inner):
            for side in range(2):
                passes = (s <= p) if side == 0 else (s >= p)

                @pl.when(jnp.logical_and(passes, has_neighbour(side)))
                def _():
                    kv_copy(side, 0, s, i, kbuf.at[s]).wait_send()
                    kv_copy(side, 1, s, i, vbuf.at[s]).wait_send()
                    z_copy(side, s, i).wait_send()
            for xx in range(chips):
                @pl.when(chip != xx)
                def _():
                    x_copy(xx, s, i).wait_send()
                sib_copy(s, xx * CORES + core, i).wait_send()
            return inner

        lax.fori_loop(0, heads, drain_head, 0)

        @pl.when(jnp.logical_not(stays(s)))
        def _():
            o_copy(s).wait_send()
        return carry

    lax.fori_loop(0, n_patch, drain, 0)


def fused_sublayer(n_patch, n_head, queries, fresh_keys, fresh_values, stale_keys, stale_values, out_weight):
    rows, width = queries.shape
    columns = out_weight.shape[1]
    sub = columns // n_head
    heads = width // HEAD_DIM
    bf16, dma = jnp.bfloat16, pltpu.SemaphoreType.DMA
    return pl.pallas_call(
        functools.partial(sublayer_kernel, n_patch, n_head),
        out_shape=jax.ShapeDtypeStruct((rows, columns), bf16),
        in_specs=[pl.BlockSpec(memory_space=pl.ANY)] * 6,
        out_specs=pl.BlockSpec(memory_space=pltpu.VMEM),
        scratch_shapes=[
            pltpu.VMEM((rows, width), bf16),
            pltpu.VMEM((rows, width), bf16),
            pltpu.VMEM((rows, width), bf16),
            pltpu.VMEM((heads, rows, HEAD_DIM), bf16),
            pltpu.VMEM((heads, rows, HEAD_DIM), bf16),
            pltpu.VMEM((width, columns), bf16),
            pltpu.VMEM((n_patch, heads, rows, HEAD_DIM), bf16),
            pltpu.VMEM((n_patch, heads, rows, HEAD_DIM), bf16),
            pltpu.VMEM((n_head, width, sub), bf16),
            pltpu.VMEM((n_head, width, sub), bf16),
            pltpu.VMEM((n_patch, n_head, heads, rows, HEAD_DIM), bf16),
            pltpu.VMEM((n_patch, rows, sub), bf16),
            pltpu.VMEM((n_head, rows, sub), bf16),
            pltpu.VMEM((rows, 1), jnp.float32),
            pltpu.VMEM((rows, 1), jnp.float32),
            pltpu.VMEM((rows, HEAD_DIM), jnp.float32),
            dma((2 * heads + 4,)),
            dma((2, 2, n_patch, heads)),
            dma((2, n_patch, heads)),
            dma((n_head,)),
            dma((n_head,)),
            dma((2, n_patch, heads)),
            dma((n_head // CORES, n_patch, heads)),
            dma((n_patch, n_head, heads)),
            dma((n_patch, n_head, heads)),
            dma((n_patch,)),
            dma((n_head,)),
        ],
        compiler_params=pltpu.CompilerParams(
            collective_id=0, has_side_effects=True, vmem_limit_bytes=56 * 1024 * 1024
        ),
    )(queries, fresh_keys, fresh_values, stale_keys, stale_values, out_weight)


def on_device(queries, fresh_keys, fresh_values, stale_keys, stale_values, out_weight, gate_scale):
    query_heads = head_view(queries)
    row_count = query_heads.shape[0]
    head_count = query_heads.shape[1]
    own_index = lax.axis_index("patch")
    own_start = own_index * row_count
    local = absorb(
        empty_state(row_count, head_count), block_scores(query_heads, fresh_keys), fresh_values
    )
    key_piece = lax.all_gather(stale_keys, "patch", axis=0, tiled=True)
    value_piece = lax.all_gather(stale_values, "patch", axis=0, tiled=True)
    key_count = key_piece.shape[0]
    key_step = 1024 if key_count > 1024 and key_count % 1024 == 0 else key_count

    def visit(block_index, inner):
        offset = block_index * key_step
        key_block = lax.dynamic_slice_in_dim(key_piece, offset, key_step, 0)
        value_block = lax.dynamic_slice_in_dim(value_piece, offset, key_step, 0)
        scores = block_scores(query_heads, key_block)
        position = offset + lax.iota(jnp.int32, key_step)
        own_rows = (position >= own_start) & (position < own_start + row_count)
        scores = jnp.where(own_rows[None, None, :], neg_large, scores)
        return absorb(inner, scores, value_block)

    run_max, run_total, run_acc = lax.fori_loop(0, key_count // key_step, visit, local)
    attended = (
        (run_acc / jnp.transpose(run_total)[:, :, None]).astype(jnp.bfloat16).reshape(row_count, -1)
    )
    partial_out = jnp.dot(
        attended,
        lax.all_gather(out_weight, "patch", axis=1, tiled=True),
        preferred_element_type=jnp.float32,
    )
    summed = lax.psum_scatter(partial_out, "head", scatter_dimension=1, tiled=True)
    return gate_scale[None, :] * summed


def solution(mesh):
    def fused(queries, fresh_keys, fresh_values, stale_keys, stale_values, out_weight, gate_scale):
        summed = fused_sublayer(
            n_patch, n_head, queries, fresh_keys, fresh_values, stale_keys, stale_values, out_weight
        )
        return gate_scale[None, :] * summed.astype(jnp.float32)

    n_patch, n_head = mesh.shape["patch"], mesh.shape["head"]
    square = n_patch == n_head and n_head % CORES == 0
    return jax.shard_map(
        fused if square else on_device,
        mesh=mesh,
        in_specs=(
            P(("groups", "patch"), "head"),
            P(("groups", "patch"), "head"),
            P(("groups", "patch"), "head"),
            P(("groups", "patch"), "head"),
            P(("groups", "patch"), "head"),
            P("head", "patch"),
            P(("groups", "head")),
        ),
        out_specs=P(("groups", "patch"), "head"),
        check_vma=False,
    )
```

```python
import functools

import jax
import jax.numpy as jnp
from jax import lax
from jax.experimental import pallas as pl
from jax.experimental.pallas import tpu as pltpu
from jax.sharding import PartitionSpec as P

HEAD_DIM = 128
MESH = pl.DeviceIdType.MESH
CORES = 2


neg_large = -1e30


def head_view(matrix):
    return matrix.reshape(matrix.shape[0], -1, HEAD_DIM)


def block_scores(query_heads, key_block):
    return jnp.einsum(
        "qhd,khd->hqk", query_heads, head_view(key_block), preferred_element_type=jnp.float32
    ) * HEAD_DIM ** (-0.5)


def absorb(running, scores, value_block):
    run_max, run_total, run_acc = running
    new_max = jnp.maximum(run_max, jnp.max(scores, axis=2))
    factor = jnp.exp(run_max - new_max)
    weights = jnp.exp(scores - new_max[:, :, None])
    new_total = run_total * factor + jnp.sum(weights, axis=2)
    mixture = jnp.einsum(
        "hqk,khd->qhd",
        weights.astype(jnp.bfloat16),
        head_view(value_block),
        preferred_element_type=jnp.float32,
    )
    new_acc = run_acc * jnp.transpose(factor)[:, :, None] + mixture
    return (new_max, new_total, new_acc)


def empty_state(row_count, head_count):
    return (
        jnp.full((head_count, row_count), neg_large, jnp.float32),
        jnp.zeros((head_count, row_count), jnp.float32),
        jnp.zeros((row_count, head_count, HEAD_DIM), jnp.float32),
    )


def sublayer_kernel(
    n_patch, n_head, q_hbm, fk_hbm, fv_hbm, sk_hbm, sv_hbm, w_hbm, out_ref,
    q_ref, fk_ref, fv_ref, w_ref, kbuf, vbuf, wsub, wbuf, abuf, ostage, obuf, top, total, acc,
    load, kv_send, kv_recv, w_send, w_recv, z_send, x_send, sib_send, a_recv, o_send, o_recv,
):
    g, p, h = lax.axis_index("groups"), lax.axis_index("patch"), lax.axis_index("head")
    core, chip = lax.rem(h, CORES), lax.div(h, CORES)
    sibling = h + 1 - 2 * core
    sub = wsub.shape[2]
    heads = q_ref.shape[1] // HEAD_DIM
    scale = HEAD_DIM ** (-0.5)

    barrier = pltpu.get_barrier_semaphore()
    for s in range(n_patch):
        for j in range(n_head):
            @pl.when(jnp.logical_or(p != s, h != j))
            def _():
                pl.semaphore_signal(barrier, inc=1, device_id=(g, s, j), device_id_type=MESH)
    loads = [
        pltpu.make_async_copy(src, dst, load.at[k])
        for k, (src, dst) in enumerate(
            ((w_hbm, w_ref), (q_hbm, q_ref), (fk_hbm, fk_ref), (fv_hbm, fv_ref))
        )
    ]
    for copy in loads:
        copy.start()
    pl.semaphore_wait(barrier, n_patch * n_head - 1)

    def remote(src, dst, send, recv, patch, head):
        return pltpu.make_async_remote_copy(
            src_ref=src, dst_ref=dst, send_sem=send, recv_sem=recv,
            device_id=(g, patch, head), device_id_type=MESH,
        )

    def neighbour(side):
        return p + 1 - 2 * side

    def has_neighbour(side):
        return (p < n_patch - 1) if side == 0 else (p > 0)

    def slab_at(side, d):
        return p - d if side == 0 else p + d

    def is_slab(side, d):
        return (p - d >= 0) if side == 0 else jnp.logical_and(p + d < n_patch, d >= 1)

    def kv_copy(side, which, s, src):
        buf = (kbuf, vbuf)[which]
        return remote(
            src, buf.at[s], kv_send.at[side, which, s], kv_recv.at[which, s], neighbour(side), h
        )

    for which, src in ((0, sk_hbm), (1, sv_hbm)):
        for side in range(2):
            @pl.when(has_neighbour(side))
            def _():
                kv_copy(side, which, p, src).start()

    def w_copy(j):
        return remote(wsub.at[j], wbuf.at[h], w_send.at[j], w_recv.at[h], p, j)

    loads[0].wait()
    for j in range(n_head):
        wsub[j] = w_ref[:, j * sub:(j + 1) * sub]

        @pl.when(h != j)
        def _():
            w_copy(j).start()
    wbuf[h] = wsub[h]
    for copy in loads[1:]:
        copy.wait()

    def absorb_block(keys, values, first):
        for i in range(heads):
            cols = slice(i * HEAD_DIM, (i + 1) * HEAD_DIM)
            scores = lax.dot_general(
                q_ref[:, cols], keys[:, cols], (((1,), (1,)), ((), ())),
                preferred_element_type=jnp.float32,
            )
            new_top = jnp.max(scores, axis=1, keepdims=True)
            if not first:
                old_top = top[i]
                new_top = jnp.maximum(old_top, new_top)
                factor = jnp.exp((old_top - new_top) * scale)
            weights = jnp.exp((scores - new_top) * scale)
            new_total = jnp.sum(weights, axis=1, keepdims=True)
            mixture = jnp.dot(
                weights.astype(jnp.bfloat16), values[:, cols], preferred_element_type=jnp.float32
            )
            if not first:
                new_total = new_total + total[i] * factor
                mixture = mixture + acc[i] * factor
            top[i] = new_top
            total[i] = new_total
            acc[i] = mixture

    absorb_block(fk_ref[...], fv_ref[...], True)

    def kv_step(d, carry):
        for which in range(2):
            for side in range(2):
                s = slab_at(side, d)

                @pl.when(is_slab(side, d))
                def _():
                    buf = (kbuf, vbuf)[which]
                    copy = kv_copy(side, which, s, buf.at[s])
                    copy.wait_recv()

                    @pl.when(has_neighbour(side))
                    def _():
                        copy.start()
        for side in range(2):
            s = slab_at(side, d)

            @pl.when(is_slab(side, d))
            def _():
                absorb_block(kbuf.at[s][...], vbuf.at[s][...], False)
        return carry

    lax.fori_loop(1, n_patch, kv_step, 0)

    for i in range(heads):
        abuf[p, h, :, i * HEAD_DIM:(i + 1) * HEAD_DIM] = (acc[i] / total[i]).astype(jnp.bfloat16)

    def z_copy(side, s):
        return remote(
            abuf.at[s, h], abuf.at[s, h], z_send.at[side, s], a_recv.at[s, h], neighbour(side), h
        )

    def x_copy(xx, s):
        return remote(
            abuf.at[s, h], abuf.at[s, h], x_send.at[xx, s], a_recv.at[s, h], p, xx * CORES + core
        )

    def sib_copy(s, head):
        return remote(
            abuf.at[s, head], abuf.at[s, head], sib_send.at[s, head], a_recv.at[s, head], p, sibling
        )

    def spread(s):
        for xx in range(n_head // CORES):
            @pl.when(chip != xx)
            def _():
                x_copy(xx, s).start()
        sib_copy(s, h).start()

    for side in range(2):
        @pl.when(has_neighbour(side))
        def _():
            z_copy(side, p).start()
    spread(p)

    for j in range(n_head):
        @pl.when(h != j)
        def _():
            remote(wsub.at[j], wbuf.at[j], w_send.at[j], w_recv.at[j], p, j).wait_recv()

    def o_copy(s):
        return remote(ostage.at[s], obuf.at[h], o_send.at[s], o_recv.at[h], s, p)

    def stays(s):
        return jnp.logical_and(s == p, h == p)

    def project(s):
        for xx in range(n_head // CORES):
            head = xx * CORES + 1 - core
            sib_in = remote(
                abuf.at[s, head], abuf.at[s, head], sib_send.at[s, h], a_recv.at[s, head], p, sibling
            )
            sib_in.wait_recv()
        term = jnp.dot(abuf[s, 0], wbuf[0], preferred_element_type=jnp.float32)
        for j in range(1, n_head):
            term = term + jnp.dot(abuf[s, j], wbuf[j], preferred_element_type=jnp.float32)
        ostage[s] = term.astype(jnp.bfloat16)

        @pl.when(stays(s))
        def _():
            obuf[h] = ostage[s]

        @pl.when(jnp.logical_not(stays(s)))
        def _():
            o_copy(s).start()

    def spread_step(d, carry):
        for side in range(2):
            s = slab_at(side, d)

            @pl.when(is_slab(side, d))
            def _():
                copy = z_copy(side, s)
                copy.wait_recv()

                @pl.when(has_neighbour(side))
                def _():
                    copy.start()
                spread(s)
        for side in range(2):
            s = slab_at(side, d - 1)

            @pl.when(is_slab(side, d - 1))
            def _():
                for xx in range(n_head // CORES):
                    @pl.when(chip != xx)
                    def _():
                        head = xx * CORES + core
                        remote(
                            abuf.at[s, head], abuf.at[s, head], x_send.at[xx, s],
                            a_recv.at[s, head], p, head,
                        ).wait_recv()
                        sib_copy(s, head).start()
        for side in range(2):
            s = slab_at(side, d - 1)

            @pl.when(is_slab(side, d - 1))
            def _():
                project(s)
        return carry

    lax.fori_loop(1, n_patch + 1, spread_step, 0)

    for j in range(n_head):
        @pl.when(jnp.logical_or(p != h, h != j))
        def _():
            remote(ostage.at[0], obuf.at[j], o_send.at[0], o_recv.at[j], h, j).wait_recv()
        out_ref[:, j * sub:(j + 1) * sub] = obuf[j]

    for j in range(n_head):
        @pl.when(h != j)
        def _():
            w_copy(j).wait_send()

    def drain(s, carry):
        for side in range(2):
            passes = (s <= p) if side == 0 else (s >= p)

            @pl.when(jnp.logical_and(passes, has_neighbour(side)))
            def _():
                kv_copy(side, 0, s, kbuf.at[s]).wait_send()
                kv_copy(side, 1, s, vbuf.at[s]).wait_send()
                z_copy(side, s).wait_send()
        for xx in range(n_head // CORES):
            @pl.when(chip != xx)
            def _():
                x_copy(xx, s).wait_send()
            sib_copy(s, xx * CORES + core).wait_send()

        @pl.when(jnp.logical_not(stays(s)))
        def _():
            o_copy(s).wait_send()
        return carry

    lax.fori_loop(0, n_patch, drain, 0)


def fused_sublayer(n_patch, n_head, queries, fresh_keys, fresh_values, stale_keys, stale_values, out_weight):
    rows, width = queries.shape
    columns = out_weight.shape[1]
    sub = columns // n_head
    heads = width // HEAD_DIM
    bf16, dma = jnp.bfloat16, pltpu.SemaphoreType.DMA
    return pl.pallas_call(
        functools.partial(sublayer_kernel, n_patch, n_head),
        out_shape=jax.ShapeDtypeStruct((rows, columns), bf16),
        in_specs=[pl.BlockSpec(memory_space=pl.ANY)] * 6,
        out_specs=pl.BlockSpec(memory_space=pltpu.VMEM),
        scratch_shapes=[
            pltpu.VMEM((rows, width), bf16),
            pltpu.VMEM((rows, width), bf16),
            pltpu.VMEM((rows, width), bf16),
            pltpu.VMEM((width, columns), bf16),
            pltpu.VMEM((n_patch, rows, width), bf16),
            pltpu.VMEM((n_patch, rows, width), bf16),
            pltpu.VMEM((n_head, width, sub), bf16),
            pltpu.VMEM((n_head, width, sub), bf16),
            pltpu.VMEM((n_patch, n_head, rows, width), bf16),
            pltpu.VMEM((n_patch, rows, sub), bf16),
            pltpu.VMEM((n_head, rows, sub), bf16),
            pltpu.VMEM((heads, rows, 1), jnp.float32),
            pltpu.VMEM((heads, rows, 1), jnp.float32),
            pltpu.VMEM((heads, rows, HEAD_DIM), jnp.float32),
            dma((4,)),
            dma((2, 2, n_patch)),
            dma((2, n_patch)),
            dma((n_head,)),
            dma((n_head,)),
            dma((2, n_patch)),
            dma((n_head // CORES, n_patch)),
            dma((n_patch, n_head)),
            dma((n_patch, n_head)),
            dma((n_patch,)),
            dma((n_head,)),
        ],
        compiler_params=pltpu.CompilerParams(
            collective_id=0, has_side_effects=True, vmem_limit_bytes=56 * 1024 * 1024
        ),
    )(queries, fresh_keys, fresh_values, stale_keys, stale_values, out_weight)


def on_device(queries, fresh_keys, fresh_values, stale_keys, stale_values, out_weight, gate_scale):
    query_heads = head_view(queries)
    row_count = query_heads.shape[0]
    head_count = query_heads.shape[1]
    own_index = lax.axis_index("patch")
    own_start = own_index * row_count
    local = absorb(
        empty_state(row_count, head_count), block_scores(query_heads, fresh_keys), fresh_values
    )
    key_piece = lax.all_gather(stale_keys, "patch", axis=0, tiled=True)
    value_piece = lax.all_gather(stale_values, "patch", axis=0, tiled=True)
    key_count = key_piece.shape[0]
    key_step = 1024 if key_count > 1024 and key_count % 1024 == 0 else key_count

    def visit(block_index, inner):
        offset = block_index * key_step
        key_block = lax.dynamic_slice_in_dim(key_piece, offset, key_step, 0)
        value_block = lax.dynamic_slice_in_dim(value_piece, offset, key_step, 0)
        scores = block_scores(query_heads, key_block)
        position = offset + lax.iota(jnp.int32, key_step)
        own_rows = (position >= own_start) & (position < own_start + row_count)
        scores = jnp.where(own_rows[None, None, :], neg_large, scores)
        return absorb(inner, scores, value_block)

    run_max, run_total, run_acc = lax.fori_loop(0, key_count // key_step, visit, local)
    attended = (
        (run_acc / jnp.transpose(run_total)[:, :, None]).astype(jnp.bfloat16).reshape(row_count, -1)
    )
    partial_out = jnp.dot(
        attended,
        lax.all_gather(out_weight, "patch", axis=1, tiled=True),
        preferred_element_type=jnp.float32,
    )
    summed = lax.psum_scatter(partial_out, "head", scatter_dimension=1, tiled=True)
    return gate_scale[None, :] * summed


def solution(mesh):
    def fused(queries, fresh_keys, fresh_values, stale_keys, stale_values, out_weight, gate_scale):
        summed = fused_sublayer(
            n_patch, n_head, queries, fresh_keys, fresh_values, stale_keys, stale_values, out_weight
        )
        return gate_scale[None, :] * summed.astype(jnp.float32)

    n_patch, n_head = mesh.shape["patch"], mesh.shape["head"]
    square = n_patch == n_head and n_head % CORES == 0
    return jax.shard_map(
        fused if square else on_device,
        mesh=mesh,
        in_specs=(
            P(("groups", "patch"), "head"),
            P(("groups", "patch"), "head"),
            P(("groups", "patch"), "head"),
            P(("groups", "patch"), "head"),
            P(("groups", "patch"), "head"),
            P("head", "patch"),
            P(("groups", "head")),
        ),
        out_specs=P(("groups", "patch"), "head"),
        check_vma=False,
    )
```

```python
import functools

import jax
import jax.numpy as jnp
from jax import lax
from jax.experimental import pallas as pl
from jax.experimental.pallas import tpu as pltpu
from jax.sharding import PartitionSpec as P

HEAD_DIM = 128
MESH = pl.DeviceIdType.MESH
CORES = 2
LANES = 128


neg_large = -1e30


def head_view(matrix):
    return matrix.reshape(matrix.shape[0], -1, HEAD_DIM)


def block_scores(query_heads, key_block):
    return jnp.einsum(
        "qhd,khd->hqk", query_heads, head_view(key_block), preferred_element_type=jnp.float32
    ) * HEAD_DIM ** (-0.5)


def absorb(running, scores, value_block):
    run_max, run_total, run_acc = running
    new_max = jnp.maximum(run_max, jnp.max(scores, axis=2))
    factor = jnp.exp(run_max - new_max)
    weights = jnp.exp(scores - new_max[:, :, None])
    new_total = run_total * factor + jnp.sum(weights, axis=2)
    mixture = jnp.einsum(
        "hqk,khd->qhd",
        weights.astype(jnp.bfloat16),
        head_view(value_block),
        preferred_element_type=jnp.float32,
    )
    new_acc = run_acc * jnp.transpose(factor)[:, :, None] + mixture
    return (new_max, new_total, new_acc)


def empty_state(row_count, head_count):
    return (
        jnp.full((head_count, row_count), neg_large, jnp.float32),
        jnp.zeros((head_count, row_count), jnp.float32),
        jnp.zeros((row_count, head_count, HEAD_DIM), jnp.float32),
    )


def sublayer_kernel(
    n_patch, n_head, q_hbm, fk_hbm, fv_hbm, sk_hbm, sv_hbm, w_hbm, out_ref,
    q_ref, fk_ref, fv_ref, w_ref, kbuf, vbuf, wbuf, abuf, ostage, obuf, top, total, acc,
    load, kv_send, kv_recv, w_send, w_recv, z_send, x_send, sib_send, a_recv, o_send, o_recv,
):
    g, p, h = lax.axis_index("groups"), lax.axis_index("patch"), lax.axis_index("head")
    core, chip = lax.rem(h, CORES), lax.div(h, CORES)
    sibling = h + 1 - 2 * core
    pair = w_ref.shape[1] // (n_head // CORES)
    wide = wbuf.shape[2]
    starts = [j // CORES * pair + j % CORES * wide for j in range(n_head)]
    widths = [wide if j % CORES == 0 else pair - wide for j in range(n_head)]

    def on_core(action):
        for c in range(CORES):
            @pl.when(core == c)
            def _():
                action(widths[c])
    heads = q_ref.shape[1] // HEAD_DIM
    scale = HEAD_DIM ** (-0.5)

    barrier = pltpu.get_barrier_semaphore()
    for s in range(n_patch):
        for j in range(n_head):
            @pl.when(jnp.logical_or(p != s, h != j))
            def _():
                pl.semaphore_signal(barrier, inc=1, device_id=(g, s, j), device_id_type=MESH)
    loads = [
        pltpu.make_async_copy(src, dst, load.at[k])
        for k, (src, dst) in enumerate(
            ((w_hbm, w_ref), (q_hbm, q_ref), (fk_hbm, fk_ref), (fv_hbm, fv_ref))
        )
    ]
    for copy in loads:
        copy.start()
    pl.semaphore_wait(barrier, n_patch * n_head - 1)

    def remote(src, dst, send, recv, patch, head):
        return pltpu.make_async_remote_copy(
            src_ref=src, dst_ref=dst, send_sem=send, recv_sem=recv,
            device_id=(g, patch, head), device_id_type=MESH,
        )

    def neighbour(side):
        return p + 1 - 2 * side

    def has_neighbour(side):
        return (p < n_patch - 1) if side == 0 else (p > 0)

    def slab_at(side, d):
        return p - d if side == 0 else p + d

    def is_slab(side, d):
        return (p - d >= 0) if side == 0 else jnp.logical_and(p + d < n_patch, d >= 1)

    def kv_copy(side, which, s, src):
        buf = (kbuf, vbuf)[which]
        return remote(
            src, buf.at[s], kv_send.at[side, which, s], kv_recv.at[which, s], neighbour(side), h
        )

    for which, src in ((0, sk_hbm), (1, sv_hbm)):
        for side in range(2):
            @pl.when(has_neighbour(side))
            def _():
                kv_copy(side, which, p, src).start()

    def w_part(j):
        return w_ref.at[:, starts[j]:starts[j] + widths[j]]

    def w_copy(j):
        return remote(
            w_part(j), wbuf.at[h, :, :widths[j]], w_send.at[j], w_recv.at[h], p, j
        )

    loads[0].wait()
    for j in range(n_head):
        @pl.when(h != j)
        def _():
            w_copy(j).start()

        @pl.when(h == j)
        def _():
            wbuf[j, :, :widths[j]] = w_part(j)[...]
    for copy in loads[1:]:
        copy.wait()

    def absorb_block(keys, values, first):
        for i in range(heads):
            cols = slice(i * HEAD_DIM, (i + 1) * HEAD_DIM)
            scores = lax.dot_general(
                q_ref[:, cols], keys[:, cols], (((1,), (1,)), ((), ())),
                preferred_element_type=jnp.float32,
            )
            new_top = jnp.max(scores, axis=1, keepdims=True)
            if not first:
                old_top = top[i]
                new_top = jnp.maximum(old_top, new_top)
                factor = jnp.exp((old_top - new_top) * scale)
            weights = jnp.exp((scores - new_top) * scale)
            new_total = jnp.sum(weights, axis=1, keepdims=True)
            mixture = jnp.dot(
                weights.astype(jnp.bfloat16), values[:, cols], preferred_element_type=jnp.float32
            )
            if not first:
                new_total = new_total + total[i] * factor
                mixture = mixture + acc[i] * factor
            top[i] = new_top
            total[i] = new_total
            acc[i] = mixture

    absorb_block(fk_ref[...], fv_ref[...], True)

    def kv_step(d, carry):
        for which in range(2):
            for side in range(2):
                s = slab_at(side, d)

                @pl.when(is_slab(side, d))
                def _():
                    buf = (kbuf, vbuf)[which]
                    copy = kv_copy(side, which, s, buf.at[s])
                    copy.wait_recv()

                    @pl.when(has_neighbour(side))
                    def _():
                        copy.start()
        for side in range(2):
            s = slab_at(side, d)

            @pl.when(is_slab(side, d))
            def _():
                absorb_block(kbuf.at[s][...], vbuf.at[s][...], False)
        return carry

    lax.fori_loop(1, n_patch, kv_step, 0)

    for i in range(heads):
        abuf[p, h, :, i * HEAD_DIM:(i + 1) * HEAD_DIM] = (acc[i] / total[i]).astype(jnp.bfloat16)

    def z_copy(side, s):
        return remote(
            abuf.at[s, h], abuf.at[s, h], z_send.at[side, s], a_recv.at[s, h], neighbour(side), h
        )

    def x_copy(xx, s):
        return remote(
            abuf.at[s, h], abuf.at[s, h], x_send.at[xx, s], a_recv.at[s, h], p, xx * CORES + core
        )

    def sib_copy(s, head):
        return remote(
            abuf.at[s, head], abuf.at[s, head], sib_send.at[s, head], a_recv.at[s, head], p, sibling
        )

    def spread(s):
        for xx in range(n_head // CORES):
            @pl.when(chip != xx)
            def _():
                x_copy(xx, s).start()
        sib_copy(s, h).start()

    for side in range(2):
        @pl.when(has_neighbour(side))
        def _():
            z_copy(side, p).start()
    spread(p)

    for j in range(n_head):
        @pl.when(h != j)
        def _():
            def arrived(width):
                part = wbuf.at[j, :, :width]
                remote(part, part, w_send.at[j], w_recv.at[j], p, j).wait_recv()
            on_core(arrived)

    def o_copy(s, width):
        return remote(
            ostage.at[s, :, :width], obuf.at[h, :, :width], o_send.at[s], o_recv.at[h], s, p
        )

    def stays(s):
        return jnp.logical_and(s == p, h == p)

    def project(s):
        for xx in range(n_head // CORES):
            head = xx * CORES + 1 - core
            sib_in = remote(
                abuf.at[s, head], abuf.at[s, head], sib_send.at[s, h], a_recv.at[s, head], p, sibling
            )
            sib_in.wait_recv()
        def finish(width):
            term = jnp.dot(abuf[s, 0], wbuf[0, :, :width], preferred_element_type=jnp.float32)
            for j in range(1, n_head):
                term = term + jnp.dot(
                    abuf[s, j], wbuf[j, :, :width], preferred_element_type=jnp.float32
                )
            ostage[s, :, :width] = term.astype(jnp.bfloat16)

            @pl.when(stays(s))
            def _():
                obuf[h, :, :width] = ostage[s, :, :width]

            @pl.when(jnp.logical_not(stays(s)))
            def _():
                o_copy(s, width).start()

        on_core(finish)

    def spread_step(d, carry):
        for side in range(2):
            s = slab_at(side, d)

            @pl.when(is_slab(side, d))
            def _():
                copy = z_copy(side, s)
                copy.wait_recv()

                @pl.when(has_neighbour(side))
                def _():
                    copy.start()
                spread(s)
        for side in range(2):
            s = slab_at(side, d - 1)

            @pl.when(is_slab(side, d - 1))
            def _():
                for xx in range(n_head // CORES):
                    @pl.when(chip != xx)
                    def _():
                        head = xx * CORES + core
                        remote(
                            abuf.at[s, head], abuf.at[s, head], x_send.at[xx, s],
                            a_recv.at[s, head], p, head,
                        ).wait_recv()
                        sib_copy(s, head).start()
        for side in range(2):
            s = slab_at(side, d - 1)

            @pl.when(is_slab(side, d - 1))
            def _():
                project(s)
        return carry

    lax.fori_loop(1, n_patch + 1, spread_step, 0)

    for j in range(n_head):
        @pl.when(jnp.logical_or(p != h, h != j))
        def _():
            part = obuf.at[j, :, :widths[j]]
            remote(part, part, o_send.at[0], o_recv.at[j], h, j).wait_recv()
        out_ref[:, starts[j]:starts[j] + widths[j]] = obuf[j, :, :widths[j]]

    for j in range(n_head):
        @pl.when(h != j)
        def _():
            w_copy(j).wait_send()

    def drain(s, carry):
        for side in range(2):
            passes = (s <= p) if side == 0 else (s >= p)

            @pl.when(jnp.logical_and(passes, has_neighbour(side)))
            def _():
                kv_copy(side, 0, s, kbuf.at[s]).wait_send()
                kv_copy(side, 1, s, vbuf.at[s]).wait_send()
                z_copy(side, s).wait_send()
        for xx in range(n_head // CORES):
            @pl.when(chip != xx)
            def _():
                x_copy(xx, s).wait_send()
            sib_copy(s, xx * CORES + core).wait_send()

        @pl.when(jnp.logical_not(stays(s)))
        def _():
            on_core(lambda width: o_copy(s, width).wait_send())
        return carry

    lax.fori_loop(0, n_patch, drain, 0)


def fused_sublayer(n_patch, n_head, queries, fresh_keys, fresh_values, stale_keys, stale_values, out_weight):
    rows, width = queries.shape
    columns = out_weight.shape[1]
    sub = -(-(columns // (n_head // CORES)) // (2 * LANES)) * LANES
    heads = width // HEAD_DIM
    bf16, dma = jnp.bfloat16, pltpu.SemaphoreType.DMA
    return pl.pallas_call(
        functools.partial(sublayer_kernel, n_patch, n_head),
        out_shape=jax.ShapeDtypeStruct((rows, columns), bf16),
        in_specs=[pl.BlockSpec(memory_space=pl.ANY)] * 6,
        out_specs=pl.BlockSpec(memory_space=pltpu.VMEM),
        scratch_shapes=[
            pltpu.VMEM((rows, width), bf16),
            pltpu.VMEM((rows, width), bf16),
            pltpu.VMEM((rows, width), bf16),
            pltpu.VMEM((width, columns), bf16),
            pltpu.VMEM((n_patch, rows, width), bf16),
            pltpu.VMEM((n_patch, rows, width), bf16),
            pltpu.VMEM((n_head, width, sub), bf16),
            pltpu.VMEM((n_patch, n_head, rows, width), bf16),
            pltpu.VMEM((n_patch, rows, sub), bf16),
            pltpu.VMEM((n_head, rows, sub), bf16),
            pltpu.VMEM((heads, rows, 1), jnp.float32),
            pltpu.VMEM((heads, rows, 1), jnp.float32),
            pltpu.VMEM((heads, rows, HEAD_DIM), jnp.float32),
            dma((4,)),
            dma((2, 2, n_patch)),
            dma((2, n_patch)),
            dma((n_head,)),
            dma((n_head,)),
            dma((2, n_patch)),
            dma((n_head // CORES, n_patch)),
            dma((n_patch, n_head)),
            dma((n_patch, n_head)),
            dma((n_patch,)),
            dma((n_head,)),
        ],
        compiler_params=pltpu.CompilerParams(
            collective_id=0, has_side_effects=True, vmem_limit_bytes=56 * 1024 * 1024
        ),
    )(queries, fresh_keys, fresh_values, stale_keys, stale_values, out_weight)


def on_device(queries, fresh_keys, fresh_values, stale_keys, stale_values, out_weight, gate_scale):
    query_heads = head_view(queries)
    row_count = query_heads.shape[0]
    head_count = query_heads.shape[1]
    own_index = lax.axis_index("patch")
    own_start = own_index * row_count
    local = absorb(
        empty_state(row_count, head_count), block_scores(query_heads, fresh_keys), fresh_values
    )
    key_piece = lax.all_gather(stale_keys, "patch", axis=0, tiled=True)
    value_piece = lax.all_gather(stale_values, "patch", axis=0, tiled=True)
    key_count = key_piece.shape[0]
    key_step = 1024 if key_count > 1024 and key_count % 1024 == 0 else key_count

    def visit(block_index, inner):
        offset = block_index * key_step
        key_block = lax.dynamic_slice_in_dim(key_piece, offset, key_step, 0)
        value_block = lax.dynamic_slice_in_dim(value_piece, offset, key_step, 0)
        scores = block_scores(query_heads, key_block)
        position = offset + lax.iota(jnp.int32, key_step)
        own_rows = (position >= own_start) & (position < own_start + row_count)
        scores = jnp.where(own_rows[None, None, :], neg_large, scores)
        return absorb(inner, scores, value_block)

    run_max, run_total, run_acc = lax.fori_loop(0, key_count // key_step, visit, local)
    attended = (
        (run_acc / jnp.transpose(run_total)[:, :, None]).astype(jnp.bfloat16).reshape(row_count, -1)
    )
    partial_out = jnp.dot(
        attended,
        lax.all_gather(out_weight, "patch", axis=1, tiled=True),
        preferred_element_type=jnp.float32,
    )
    summed = lax.psum_scatter(partial_out, "head", scatter_dimension=1, tiled=True)
    return gate_scale[None, :] * summed


def solution(mesh):
    def fused(queries, fresh_keys, fresh_values, stale_keys, stale_values, out_weight, gate_scale):
        summed = fused_sublayer(
            n_patch, n_head, queries, fresh_keys, fresh_values, stale_keys, stale_values, out_weight
        )
        return gate_scale[None, :] * summed.astype(jnp.float32)

    n_patch, n_head = mesh.shape["patch"], mesh.shape["head"]
    square = n_patch == n_head and n_head % CORES == 0
    return jax.shard_map(
        fused if square else on_device,
        mesh=mesh,
        in_specs=(
            P(("groups", "patch"), "head"),
            P(("groups", "patch"), "head"),
            P(("groups", "patch"), "head"),
            P(("groups", "patch"), "head"),
            P(("groups", "patch"), "head"),
            P("head", "patch"),
            P(("groups", "head")),
        ),
        out_specs=P(("groups", "patch"), "head"),
        check_vma=False,
    )
```

```python
import functools

import jax
import jax.numpy as jnp
from jax import lax
from jax.experimental import pallas as pl
from jax.experimental.pallas import tpu as pltpu
from jax.sharding import PartitionSpec as P

HEAD_DIM = 128
MESH = pl.DeviceIdType.MESH
CORES = 2
LANES = 128


neg_large = -1e30


def head_view(matrix):
    return matrix.reshape(matrix.shape[0], -1, HEAD_DIM)


def block_scores(query_heads, key_block):
    return jnp.einsum(
        "qhd,khd->hqk", query_heads, head_view(key_block), preferred_element_type=jnp.float32
    ) * HEAD_DIM ** (-0.5)


def absorb(running, scores, value_block):
    run_max, run_total, run_acc = running
    new_max = jnp.maximum(run_max, jnp.max(scores, axis=2))
    factor = jnp.exp(run_max - new_max)
    weights = jnp.exp(scores - new_max[:, :, None])
    new_total = run_total * factor + jnp.sum(weights, axis=2)
    mixture = jnp.einsum(
        "hqk,khd->qhd",
        weights.astype(jnp.bfloat16),
        head_view(value_block),
        preferred_element_type=jnp.float32,
    )
    new_acc = run_acc * jnp.transpose(factor)[:, :, None] + mixture
    return (new_max, new_total, new_acc)


def empty_state(row_count, head_count):
    return (
        jnp.full((head_count, row_count), neg_large, jnp.float32),
        jnp.zeros((head_count, row_count), jnp.float32),
        jnp.zeros((row_count, head_count, HEAD_DIM), jnp.float32),
    )


def sublayer_kernel(
    n_patch, n_head, q_hbm, fk_hbm, fv_hbm, sk_hbm, sv_hbm, w_hbm, out_ref,
    q_ref, fk_ref, fv_ref, kbuf, vbuf, wbuf, abuf, ostage, obuf, top, total, acc,
    load, kv_send, kv_recv, w_send, w_recv, z_send, x_send, sib_send, a_recv, o_send, o_recv,
):
    g, p, h = lax.axis_index("groups"), lax.axis_index("patch"), lax.axis_index("head")
    core, chip = lax.rem(h, CORES), lax.div(h, CORES)
    sibling = h + 1 - 2 * core
    pair = w_hbm.shape[1] // (n_head // CORES)
    wide = wbuf.shape[2]
    starts = [j // CORES * pair + j % CORES * wide for j in range(n_head)]
    widths = [wide if j % CORES == 0 else pair - wide for j in range(n_head)]

    def on_core(action):
        for c in range(CORES):
            @pl.when(core == c)
            def _():
                action(widths[c])
    heads = q_ref.shape[1] // HEAD_DIM
    scale = HEAD_DIM ** (-0.5)

    barrier = pltpu.get_barrier_semaphore()
    for s in range(n_patch):
        for j in range(n_head):
            @pl.when(jnp.logical_or(p != s, h != j))
            def _():
                pl.semaphore_signal(barrier, inc=1, device_id=(g, s, j), device_id_type=MESH)
    loads = [
        pltpu.make_async_copy(src, dst, load.at[k])
        for k, (src, dst) in enumerate(
            ((q_hbm, q_ref), (fk_hbm, fk_ref), (fv_hbm, fv_ref))
        )
    ]
    for copy in loads:
        copy.start()
    pl.semaphore_wait(barrier, n_patch * n_head - 1)

    def remote(src, dst, send, recv, patch, head):
        return pltpu.make_async_remote_copy(
            src_ref=src, dst_ref=dst, send_sem=send, recv_sem=recv,
            device_id=(g, patch, head), device_id_type=MESH,
        )

    def neighbour(side):
        return p + 1 - 2 * side

    def has_neighbour(side):
        return (p < n_patch - 1) if side == 0 else (p > 0)

    def slab_at(side, d):
        return p - d if side == 0 else p + d

    def is_slab(side, d):
        return (p - d >= 0) if side == 0 else jnp.logical_and(p + d < n_patch, d >= 1)

    def kv_copy(side, which, s, src):
        buf = (kbuf, vbuf)[which]
        return remote(
            src, buf.at[s], kv_send.at[side, which, s], kv_recv.at[which, s], neighbour(side), h
        )

    for which, src in ((0, sk_hbm), (1, sv_hbm)):
        for side in range(2):
            @pl.when(has_neighbour(side))
            def _():
                kv_copy(side, which, p, src).start()

    def w_part(j):
        return w_hbm.at[:, starts[j]:starts[j] + widths[j]]

    def w_own(j):
        return pltpu.make_async_copy(w_part(j), wbuf.at[j, :, :widths[j]], w_send.at[j])

    def w_copy(j):
        return remote(
            w_part(j), wbuf.at[h, :, :widths[j]], w_send.at[j], w_recv.at[h], p, j
        )

    for j in range(n_head):
        @pl.when(h != j)
        def _():
            w_copy(j).start()

        @pl.when(h == j)
        def _():
            w_own(j).start()
    for copy in loads:
        copy.wait()

    def absorb_block(keys, values, first):
        for i in range(heads):
            cols = slice(i * HEAD_DIM, (i + 1) * HEAD_DIM)
            scores = lax.dot_general(
                q_ref[:, cols], keys[:, cols], (((1,), (1,)), ((), ())),
                preferred_element_type=jnp.float32,
            )
            new_top = jnp.max(scores, axis=1, keepdims=True)
            if not first:
                old_top = top[i]
                new_top = jnp.maximum(old_top, new_top)
                factor = jnp.exp((old_top - new_top) * scale)
            weights = jnp.exp((scores - new_top) * scale)
            new_total = jnp.sum(weights, axis=1, keepdims=True)
            mixture = jnp.dot(
                weights.astype(jnp.bfloat16), values[:, cols], preferred_element_type=jnp.float32
            )
            if not first:
                new_total = new_total + total[i] * factor
                mixture = mixture + acc[i] * factor
            top[i] = new_top
            total[i] = new_total
            acc[i] = mixture

    absorb_block(fk_ref[...], fv_ref[...], True)

    def kv_step(d, carry):
        for which in range(2):
            for side in range(2):
                s = slab_at(side, d)

                @pl.when(is_slab(side, d))
                def _():
                    buf = (kbuf, vbuf)[which]
                    copy = kv_copy(side, which, s, buf.at[s])
                    copy.wait_recv()

                    @pl.when(has_neighbour(side))
                    def _():
                        copy.start()
        for side in range(2):
            s = slab_at(side, d)

            @pl.when(is_slab(side, d))
            def _():
                absorb_block(kbuf.at[s][...], vbuf.at[s][...], False)
        return carry

    lax.fori_loop(1, n_patch, kv_step, 0)

    for i in range(heads):
        abuf[p, h, :, i * HEAD_DIM:(i + 1) * HEAD_DIM] = (acc[i] / total[i]).astype(jnp.bfloat16)

    def z_copy(side, s):
        return remote(
            abuf.at[s, h], abuf.at[s, h], z_send.at[side, s], a_recv.at[s, h], neighbour(side), h
        )

    def x_copy(xx, s):
        return remote(
            abuf.at[s, h], abuf.at[s, h], x_send.at[xx, s], a_recv.at[s, h], p, xx * CORES + core
        )

    def sib_copy(s, head):
        return remote(
            abuf.at[s, head], abuf.at[s, head], sib_send.at[s, head], a_recv.at[s, head], p, sibling
        )

    def spread(s):
        for xx in range(n_head // CORES):
            @pl.when(chip != xx)
            def _():
                x_copy(xx, s).start()
        sib_copy(s, h).start()

    for side in range(2):
        @pl.when(has_neighbour(side))
        def _():
            z_copy(side, p).start()
    spread(p)

    for j in range(n_head):
        @pl.when(h != j)
        def _():
            def arrived(width):
                part = wbuf.at[j, :, :width]
                remote(part, part, w_send.at[j], w_recv.at[j], p, j).wait_recv()
            on_core(arrived)

        @pl.when(h == j)
        def _():
            w_own(j).wait()

    def o_copy(s, width):
        return remote(
            ostage.at[s, :, :width], obuf.at[h, :, :width], o_send.at[s], o_recv.at[h], s, p
        )

    def stays(s):
        return jnp.logical_and(s == p, h == p)

    def project(s):
        for xx in range(n_head // CORES):
            head = xx * CORES + 1 - core
            sib_in = remote(
                abuf.at[s, head], abuf.at[s, head], sib_send.at[s, h], a_recv.at[s, head], p, sibling
            )
            sib_in.wait_recv()
        def finish(width):
            term = jnp.dot(abuf[s, 0], wbuf[0, :, :width], preferred_element_type=jnp.float32)
            for j in range(1, n_head):
                term = term + jnp.dot(
                    abuf[s, j], wbuf[j, :, :width], preferred_element_type=jnp.float32
                )
            ostage[s, :, :width] = term.astype(jnp.bfloat16)

            @pl.when(stays(s))
            def _():
                obuf[h, :, :width] = ostage[s, :, :width]

            @pl.when(jnp.logical_not(stays(s)))
            def _():
                o_copy(s, width).start()

        on_core(finish)

    def spread_step(d, carry):
        for side in range(2):
            s = slab_at(side, d)

            @pl.when(is_slab(side, d))
            def _():
                copy = z_copy(side, s)
                copy.wait_recv()

                @pl.when(has_neighbour(side))
                def _():
                    copy.start()
                spread(s)
        for side in range(2):
            s = slab_at(side, d - 1)

            @pl.when(is_slab(side, d - 1))
            def _():
                for xx in range(n_head // CORES):
                    @pl.when(chip != xx)
                    def _():
                        head = xx * CORES + core
                        remote(
                            abuf.at[s, head], abuf.at[s, head], x_send.at[xx, s],
                            a_recv.at[s, head], p, head,
                        ).wait_recv()
                        sib_copy(s, head).start()
        for side in range(2):
            s = slab_at(side, d - 1)

            @pl.when(is_slab(side, d - 1))
            def _():
                project(s)
        return carry

    lax.fori_loop(1, n_patch + 1, spread_step, 0)

    for j in range(n_head):
        @pl.when(jnp.logical_or(p != h, h != j))
        def _():
            part = obuf.at[j, :, :widths[j]]
            remote(part, part, o_send.at[0], o_recv.at[j], h, j).wait_recv()
        out_ref[:, starts[j]:starts[j] + widths[j]] = obuf[j, :, :widths[j]]

    for j in range(n_head):
        @pl.when(h != j)
        def _():
            w_copy(j).wait_send()

    def drain(s, carry):
        for side in range(2):
            passes = (s <= p) if side == 0 else (s >= p)

            @pl.when(jnp.logical_and(passes, has_neighbour(side)))
            def _():
                kv_copy(side, 0, s, kbuf.at[s]).wait_send()
                kv_copy(side, 1, s, vbuf.at[s]).wait_send()
                z_copy(side, s).wait_send()
        for xx in range(n_head // CORES):
            @pl.when(chip != xx)
            def _():
                x_copy(xx, s).wait_send()
            sib_copy(s, xx * CORES + core).wait_send()

        @pl.when(jnp.logical_not(stays(s)))
        def _():
            on_core(lambda width: o_copy(s, width).wait_send())
        return carry

    lax.fori_loop(0, n_patch, drain, 0)


def fused_sublayer(n_patch, n_head, queries, fresh_keys, fresh_values, stale_keys, stale_values, out_weight):
    rows, width = queries.shape
    columns = out_weight.shape[1]
    sub = -(-(columns // (n_head // CORES)) // (2 * LANES)) * LANES
    heads = width // HEAD_DIM
    bf16, dma = jnp.bfloat16, pltpu.SemaphoreType.DMA
    return pl.pallas_call(
        functools.partial(sublayer_kernel, n_patch, n_head),
        out_shape=jax.ShapeDtypeStruct((rows, columns), bf16),
        in_specs=[pl.BlockSpec(memory_space=pl.ANY)] * 6,
        out_specs=pl.BlockSpec(memory_space=pltpu.VMEM),
        scratch_shapes=[
            pltpu.VMEM((rows, width), bf16),
            pltpu.VMEM((rows, width), bf16),
            pltpu.VMEM((rows, width), bf16),
            pltpu.VMEM((n_patch, rows, width), bf16),
            pltpu.VMEM((n_patch, rows, width), bf16),
            pltpu.VMEM((n_head, width, sub), bf16),
            pltpu.VMEM((n_patch, n_head, rows, width), bf16),
            pltpu.VMEM((n_patch, rows, sub), bf16),
            pltpu.VMEM((n_head, rows, sub), bf16),
            pltpu.VMEM((heads, rows, 1), jnp.float32),
            pltpu.VMEM((heads, rows, 1), jnp.float32),
            pltpu.VMEM((heads, rows, HEAD_DIM), jnp.float32),
            dma((3,)),
            dma((2, 2, n_patch)),
            dma((2, n_patch)),
            dma((n_head,)),
            dma((n_head,)),
            dma((2, n_patch)),
            dma((n_head // CORES, n_patch)),
            dma((n_patch, n_head)),
            dma((n_patch, n_head)),
            dma((n_patch,)),
            dma((n_head,)),
        ],
        compiler_params=pltpu.CompilerParams(
            collective_id=0, has_side_effects=True, vmem_limit_bytes=56 * 1024 * 1024
        ),
    )(queries, fresh_keys, fresh_values, stale_keys, stale_values, out_weight)


def on_device(queries, fresh_keys, fresh_values, stale_keys, stale_values, out_weight, gate_scale):
    query_heads = head_view(queries)
    row_count = query_heads.shape[0]
    head_count = query_heads.shape[1]
    own_index = lax.axis_index("patch")
    own_start = own_index * row_count
    local = absorb(
        empty_state(row_count, head_count), block_scores(query_heads, fresh_keys), fresh_values
    )
    key_piece = lax.all_gather(stale_keys, "patch", axis=0, tiled=True)
    value_piece = lax.all_gather(stale_values, "patch", axis=0, tiled=True)
    key_count = key_piece.shape[0]
    key_step = 1024 if key_count > 1024 and key_count % 1024 == 0 else key_count

    def visit(block_index, inner):
        offset = block_index * key_step
        key_block = lax.dynamic_slice_in_dim(key_piece, offset, key_step, 0)
        value_block = lax.dynamic_slice_in_dim(value_piece, offset, key_step, 0)
        scores = block_scores(query_heads, key_block)
        position = offset + lax.iota(jnp.int32, key_step)
        own_rows = (position >= own_start) & (position < own_start + row_count)
        scores = jnp.where(own_rows[None, None, :], neg_large, scores)
        return absorb(inner, scores, value_block)

    run_max, run_total, run_acc = lax.fori_loop(0, key_count // key_step, visit, local)
    attended = (
        (run_acc / jnp.transpose(run_total)[:, :, None]).astype(jnp.bfloat16).reshape(row_count, -1)
    )
    partial_out = jnp.dot(
        attended,
        lax.all_gather(out_weight, "patch", axis=1, tiled=True),
        preferred_element_type=jnp.float32,
    )
    summed = lax.psum_scatter(partial_out, "head", scatter_dimension=1, tiled=True)
    return gate_scale[None, :] * summed


def solution(mesh):
    def fused(queries, fresh_keys, fresh_values, stale_keys, stale_values, out_weight, gate_scale):
        summed = fused_sublayer(
            n_patch, n_head, queries, fresh_keys, fresh_values, stale_keys, stale_values, out_weight
        )
        return gate_scale[None, :] * summed.astype(jnp.float32)

    n_patch, n_head = mesh.shape["patch"], mesh.shape["head"]
    square = n_patch == n_head and n_head % CORES == 0
    return jax.shard_map(
        fused if square else on_device,
        mesh=mesh,
        in_specs=(
            P(("groups", "patch"), "head"),
            P(("groups", "patch"), "head"),
            P(("groups", "patch"), "head"),
            P(("groups", "patch"), "head"),
            P(("groups", "patch"), "head"),
            P("head", "patch"),
            P(("groups", "head")),
        ),
        out_specs=P(("groups", "patch"), "head"),
        check_vma=False,
    )
```
